32 devices in a mesh: section: 2 (over core), wide: 16 (over z, y, x).
Axes of the slice: x: 2, y: 2, z: 4, core: 2. Of those that a mesh axis runs over, the one named last changes fastest.
Arguments:
- inputs: bfloat16 [2, 16, 256, 1024], P(None, 'wide'), may hold values from -6 to 6
- memories: bfloat16 [2, 2, 16, 128, 1024], P('section', None, 'wide'), may hold values from -6 to 6
- cmems: bfloat16 [2, 2, 16, 128, 1024], P('section', None, 'wide'), may hold values from -6 to 6
- cotangent: bfloat16 [2, 16, 256, 1024], P(None, 'wide'), may hold values from -6 to 6
- q_weight: bfloat16 [2, 1024, 1024], P('section', 'wide'), may hold values from -0.1875 to 0.1875
- key_weight: bfloat16 [2, 1024, 1024], P('section', 'wide'), may hold values from -0.1875 to 0.1875
- value_weight: bfloat16 [2, 1024, 1024], P('section', 'wide'), may hold values from -0.1875 to 0.1875
- pos_weight: bfloat16 [2, 1024, 1024], P('section', 'wide'), may hold values from -0.1875 to 0.1875
- out_weight: bfloat16 [2, 1024, 1024], P('section', 'wide'), may hold values from -3 to 3
- up_weight: bfloat16 [2, 1024, 4096], P('section', 'wide'), may hold values from -0.1875 to 0.1875
- down_weight: bfloat16 [2, 4096, 1024], P('section', 'wide'), may hold values from -0.09375 to 0.09375
- comp_weight: bfloat16 [2, 3, 1024, 1024], P('section', None, 'wide'), may hold values from -0.109375 to 0.109375
- norm_gain: bfloat16 [2, 1024], P('section', 'wide'), may hold values from 0.5 to 1.5
- content_bias: bfloat16 [2, 1024], P('section', 'wide'), may hold values from -3 to 3
- position_bias: bfloat16 [2, 1024], P('section', 'wide'), may hold values from -3 to 3
- ffn_gain: bfloat16 [2, 1024], P('section', 'wide'), may hold values from 0.5 to 1.5
- up_bias: bfloat16 [2, 4096], P('section', 'wide'), may hold values from -3 to 3
- down_bias: bfloat16 [2, 1024], P('section', 'wide'), may hold values from -3 to 3
Outputs:
- activations: bfloat16 [2, 2, 16, 256, 1024], P('section', None, 'wide')
- input_grads: float32 [2, 2, 16, 256, 1024], P('section', None, 'wide')
- q_grad: float32 [2, 1024, 1024], P('section', 'wide')
- key_grad: float32 [2, 1024, 1024], P('section', 'wide')
- value_grad: float32 [2, 1024, 1024], P('section', 'wide')
- pos_grad: float32 [2, 1024, 1024], P('section', 'wide')
- out_grad: float32 [2, 1024, 1024], P('section', 'wide')
- up_grad: float32 [2, 1024, 4096], P('section', 'wide')
- down_grad: float32 [2, 4096, 1024], P('section', 'wide')
- comp_grad: float32 [2, 3, 1024, 1024], P('section', None, 'wide')
- norm_gain_grad: float32 [2, 1024], P('section', 'wide')
- content_bias_grad: float32 [2, 1024], P('section', 'wide')
- position_bias_grad: float32 [2, 1024], P('section', 'wide')
- ffn_gain_grad: float32 [2, 1024], P('section', 'wide')
- up_bias_grad: float32 [2, 4096], P('section', 'wide')
- down_bias_grad: float32 [2, 1024], P('section', 'wide')
The draws below stay inside these ranges and needn't reach their ends.
All inputs are finite; a program needn't handle non-finite values.
Results may differ from the reference program's by a relative error of at most 0.023.
Values may be sent and summed in bfloat16 or wider, within the bound.
No kernel may reach another device: no remote copies, remote signals or barrier semaphores. Data moves between devices by JAX's collectives and lax.ppermute only.
A program may use at most 320 MiB of HBM per device.

```python
import jax
import jax.numpy as jnp
from jax import lax

D = 1024
HEAD_COUNT = 8
HEAD_WIDTH = 128
FF = 4096
MEM = 128
CMEM = 128
SEG = 256
CNEW = 32
MICRO = 2
LAYERS = 2
STR_DEV = 1
STREAMS = 16
VISIBLE_KEYS = 512
N_WIDE = 16


def steps_of(key, extent, cuts, least, largest):
    factor_of = 1.0
    for axis_at, shards_of in cuts:
        draws = jax.random.uniform(jax.random.fold_in(jax.random.fold_in(key, 6), axis_at), (shards_of,), jnp.float32, least / len(cuts), largest / len(cuts))
        factor_of = factor_of * jnp.repeat(jnp.exp(draws), extent[axis_at] // shards_of).reshape((-1,) + (1,) * (len(extent) - 1 - axis_at))
    return factor_of


def scatter_about(own_key, extent, spread, bound, shards=(), held_as=jnp.bfloat16):
    result = jax.random.normal(own_key, extent, jnp.float32) * spread
    if len(shards) > 0:
        result = steps_of(own_key, extent, shards, -0.22, 0.18) * result
    return jnp.clip(result, min=-bound, max=bound).astype(held_as)


def setup_inputs(seed: int = 0) -> dict:
    keys = jax.random.split(jax.random.key(seed), 19)
    return {
        "inputs": scatter_about(keys[0], (MICRO, STREAMS, SEG, D), 1.0, 6.0, ((1, 16),)),
        "memories": scatter_about(keys[1], (LAYERS, MICRO, STREAMS, MEM, D), 1.0, 6.0, ((0, 2), (2, 16))),
        "cmems": scatter_about(keys[2], (LAYERS, MICRO, STREAMS, CMEM, D), 1.0, 6.0, ((0, 2), (2, 16))),
        "cotangent": scatter_about(keys[3], (MICRO, STREAMS, SEG, D), 1.0, 6.0, ((1, 16),)),
        "q_weight": scatter_about(keys[4], (LAYERS, D, D), D ** -0.5, 0.1875, ((0, 2), (1, 16))),
        "key_weight": scatter_about(keys[5], (LAYERS, D, D), D ** -0.5, 0.1875, ((0, 2), (1, 16))),
        "value_weight": scatter_about(keys[6], (LAYERS, D, D), D ** -0.5, 0.1875, ((0, 2), (1, 16))),
        "pos_weight": scatter_about(keys[7], (LAYERS, D, D), D ** -0.5, 0.1875, ((0, 2), (1, 16))),
        "out_weight": scatter_about(keys[8], (LAYERS, D, D), (max(D // 256, 1)) ** -0.5, 3.0, ((0, 2), (1, 16))),
        "up_weight": scatter_about(keys[9], (LAYERS, D, FF), D ** -0.5, 0.1875, ((0, 2), (1, 16))),
        "down_weight": scatter_about(keys[10], (LAYERS, FF, D), FF ** -0.5, 0.09375, ((0, 2), (1, 16))),
        "comp_weight": scatter_about(keys[11], (LAYERS, 3, D, D), (3 * D) ** -0.5, 0.109375, ((0, 2), (2, 16))),
        "norm_gain": jnp.clip(1.0 + 0.1 * jax.random.normal(keys[12], (LAYERS, D), jnp.float32), 0.5, 1.5).astype(jnp.bfloat16),
        "content_bias": scatter_about(keys[13], (LAYERS, D), 0.5, 3.0, ((0, 2), (1, 16))),
        "position_bias": scatter_about(keys[14], (LAYERS, D), 0.5, 3.0, ((0, 2), (1, 16))),
        "ffn_gain": jnp.clip(1.0 + 0.1 * jax.random.normal(keys[15], (LAYERS, D), jnp.float32), 0.5, 1.5).astype(jnp.bfloat16),
        "up_bias": scatter_about(keys[16], (LAYERS, FF), 0.5, 3.0, ((0, 2), (1, 16))),
        "down_bias": scatter_about(keys[17], (LAYERS, D), 0.5, 3.0, ((0, 2), (1, 16))),
    }


@jax.custom_vjp
def lowered_rows(v):
    return lax.optimization_barrier(v.astype(jnp.bfloat16)).astype(jnp.float32)

@jax.custom_vjp
def lowered_backward(v):
    return v

def low_keep(v):
    return (lowered_rows(v), None)

def low_pass(kept, grad):
    return (grad,)

def back_keep(v):
    return (v, None)

def back_low(kept, grad):
    return (lowered_rows(grad),)
lowered_rows.defvjp(low_keep, low_pass)
lowered_backward.defvjp(back_keep, back_low)
highest = lax.Precision.HIGHEST
epsilon = 1e-05

def einsum_product(pattern, left_op, right_op):
    return jnp.einsum(pattern, left_op, right_op, precision=highest, preferred_element_type=jnp.float32)

def relative_table():
    distance = (VISIBLE_KEYS - 1 - jnp.arange(VISIBLE_KEYS)).astype(jnp.float32)
    inv_freq = 1.0 / 10000.0 ** (jnp.arange(0, D, 2).astype(jnp.float32) / D)
    angles = distance[:, None] * inv_freq[None, :]
    return jnp.concatenate([jnp.sin(angles), jnp.cos(angles)], axis=1)

def normalize(rows_in, gain_in):
    average = lax.optimization_barrier(jnp.mean(rows_in, -1, keepdims=True))
    centered = rows_in - average
    variance = lax.optimization_barrier(jnp.mean(centered * centered, -1, keepdims=True))
    return centered * lax.rsqrt(variance + epsilon) * gain_in

def attention_layer(params, layer_in, memory, compressed, rel_base):
    w_query, key_projection, value_projection, w_pos, w_out, w_up, w_down, gain_norm, bias_content, bias_position, gain_ffn, bias_up, bias_down = params
    current_stream_count = layer_in.shape[0]
    scale_query = HEAD_WIDTH ** (-0.5)
    allrows = jnp.concatenate([compressed, memory, layer_in], axis=1)
    context_rows = lowered_rows(normalize(allrows, gain_norm))
    current = context_rows[:, CMEM + MEM:]
    query_proj = lowered_backward(einsum_product('bsd,de->bse', current, w_query))
    q_content = lowered_rows((query_proj + bias_content) * scale_query).reshape(current_stream_count, SEG, HEAD_COUNT, HEAD_WIDTH)
    q_position = lowered_rows((query_proj + bias_position) * scale_query).reshape(current_stream_count, SEG, HEAD_COUNT, HEAD_WIDTH)
    every_key_row = lowered_rows(lowered_backward(einsum_product('pty,ya->pta', context_rows, key_projection))).reshape(current_stream_count, VISIBLE_KEYS, HEAD_COUNT, HEAD_WIDTH)
    every_value_row = lowered_rows(lowered_backward(einsum_product('pty,ya->pta', context_rows, value_projection))).reshape(current_stream_count, VISIBLE_KEYS, HEAD_COUNT, HEAD_WIDTH)
    rel_keys = lowered_rows(lowered_backward(jnp.broadcast_to(rel_base[None], (current_stream_count, VISIBLE_KEYS, D)))).reshape(current_stream_count, VISIBLE_KEYS, HEAD_COUNT, HEAD_WIDTH)
    content_scores = einsum_product('bihd,bjhd->bhij', q_content, every_key_row)
    table_scores = einsum_product('bihd,bphd->bhip', q_position, rel_keys)
    row_index = lax.broadcasted_iota(jnp.int32, (SEG, VISIBLE_KEYS), 0)
    col_index = lax.broadcasted_iota(jnp.int32, (SEG, VISIBLE_KEYS), 1)
    gather_index = jnp.minimum(SEG - 1 - row_index + col_index, VISIBLE_KEYS - 1).astype(jnp.int32)
    position_scores = jnp.take_along_axis(table_scores, jnp.broadcast_to(gather_index, table_scores.shape), axis=3)
    scores = lowered_backward(content_scores + position_scores)
    scores = jnp.where(col_index <= row_index + (CMEM + MEM), scores, -1e+30)
    attention = lowered_rows(jax.nn.softmax(scores, axis=-1))
    mixed_heads = lowered_rows(lowered_backward(einsum_product('bhij,bjhd->bihd', attention, every_value_row))).reshape(current_stream_count, SEG, D)
    middle = layer_in + lowered_backward(einsum_product('bsd,de->bse', mixed_heads, w_out))
    ffn_in = lowered_rows(normalize(middle, gain_ffn))
    pre_act = lowered_backward(einsum_product('bsd,df->bsf', ffn_in, w_up) + bias_up)
    hidden = lowered_rows(jax.nn.gelu(pre_act, approximate=False))
    return middle + lowered_backward(einsum_product('bsf,fd->bsd', hidden, w_down)) + bias_down

def compress_loss(w_comp, memory):
    current_stream_count = memory.shape[0]
    oldest = memory[:, :3 * CNEW].reshape(current_stream_count, CNEW, 3 * D)
    comp_flat = w_comp.reshape(3 * D, D)
    squeezed = lowered_rows(lowered_backward(einsum_product('bnk,kd->bnd', oldest, comp_flat)))
    rebuilt = lowered_backward(einsum_product('bnd,kd->bnk', squeezed, comp_flat))
    residue = rebuilt - oldest
    return jnp.sum(residue * residue) / (3 * CNEW)

def forward_all(all_params, comp_all, inputs_grp, memory_grp, compressed_grp, inject):
    table_low = lowered_rows(relative_table())
    outputs_all = []
    recon_loss = jnp.zeros((), jnp.float32)
    current_in = inputs_grp
    for layer_idx in range(LAYERS):
        params = all_params[layer_idx]
        rel_base = einsum_product('pd,de->pe', table_low, params[3])
        results = []
        for micro_idx in range(MICRO):
            layer_in = current_in[micro_idx] + inject[layer_idx, micro_idx]
            results.append(attention_layer(params, layer_in, memory_grp[layer_idx, micro_idx], compressed_grp[layer_idx, micro_idx], rel_base))
            recon_loss = recon_loss + compress_loss(comp_all[layer_idx], memory_grp[layer_idx, micro_idx])
        stacked = jnp.stack(results)
        if layer_idx + 1 < LAYERS:
            stacked = lowered_rows(lowered_backward(stacked))
        outputs_all.append(stacked)
        current_in = stacked
    return (jnp.stack(outputs_all), recon_loss)

def reference(inputs, memories, cmems, cotangent, q_weight, key_weight, value_weight, pos_weight, out_weight, up_weight, down_weight, comp_weight, norm_gain, content_bias, position_bias, ffn_gain, up_bias, down_bias):
    matrices = [source.astype(jnp.float32) for source in (q_weight, key_weight, value_weight, pos_weight, out_weight, up_weight, down_weight, norm_gain, content_bias, position_bias, ffn_gain, up_bias, down_bias)]
    all_params = tuple((tuple((source[layer_idx] for source in matrices)) for layer_idx in range(LAYERS)))
    comp_all = comp_weight.astype(jnp.float32)
    inputs_f = inputs.astype(jnp.float32)
    memories_f = memories.astype(jnp.float32)
    cmems_f = cmems.astype(jnp.float32)
    cotangent_f = cotangent.astype(jnp.float32)

    def group_step(totals, group_index):
        group_start = group_index * STR_DEV
        inputs_grp = lax.dynamic_slice_in_dim(inputs_f, group_start, STR_DEV, 1)
        memory_grp = lax.dynamic_slice_in_dim(memories_f, group_start, STR_DEV, 2)
        compressed_grp = lax.dynamic_slice_in_dim(cmems_f, group_start, STR_DEV, 2)
        cot_grp = lax.dynamic_slice_in_dim(cotangent_f, group_start, STR_DEV, 1)
        inject = jnp.zeros((LAYERS,) + inputs_grp.shape, jnp.float32)

        def wrapped(params_in, comp_in, inject_in):
            return forward_all(params_in, comp_in, inputs_grp, memory_grp, compressed_grp, inject_in)
        (outputs_all, recon_loss), pullback = jax.vjp(wrapped, all_params, comp_all, inject)
        cot_full = jnp.zeros_like(outputs_all).at[LAYERS - 1].set(cot_grp)
        grad_params, grad_comp, grad_inject = pullback((cot_full, jnp.ones_like(recon_loss)))
        totals = jax.tree.map(jnp.add, totals, (grad_params, grad_comp))
        return (totals, (outputs_all, grad_inject))
    zeros_init = jax.tree.map(jnp.zeros_like, (all_params, comp_all))
    totals, (outputs_all, grad_inject) = lax.scan(group_step, zeros_init, jnp.arange(N_WIDE, dtype=jnp.int32))
    grad_params, grad_comp = totals
    acts_out = jnp.transpose(outputs_all, (1, 2, 0, 3, 4, 5)).reshape(LAYERS, MICRO, STREAMS, SEG, D)
    grads_in = jnp.transpose(grad_inject, (1, 2, 0, 3, 4, 5)).reshape(LAYERS, MICRO, STREAMS, SEG, D)
    stacked_grads = [jnp.stack([grad_params[layer_idx][pick] for layer_idx in range(LAYERS)]) for pick in range(13)]
    return (acts_out.astype(jnp.bfloat16), grads_in, stacked_grads[0], stacked_grads[1], stacked_grads[2], stacked_grads[3], stacked_grads[4], stacked_grads[5], stacked_grads[6], grad_comp, stacked_grads[7], stacked_grads[8], stacked_grads[9], stacked_grads[10], stacked_grads[11], stacked_grads[12])
```

```python
import jax
import jax.numpy as jnp
from jax import lax
from jax.sharding import PartitionSpec as P

HEADS = 8
HEAD_WIDTH = 128
MEM = 128
CMEM = 128
SEG = 256
CNEW = 32
VISIBLE_KEYS = 512
EPSILON = 1e-05
SCALE = HEAD_WIDTH ** (-0.5)
BF = jnp.bfloat16
F32 = jnp.float32


class Places:
    def __init__(self):
        self.n = lax.axis_size("wide")
        self.quarter = self.n // 4
        self.pair = self.quarter
        self.zmask = 3 * self.quarter
        self.low = []
        bit = 1
        while bit < self.quarter:
            self.low.append(bit)
            bit *= 2
        self.wide = lax.axis_index("wide")
        self.core = lax.axis_index("section")
        self.layer = self.layer_of(self.wide)
        self.first = self.layer == 0
        self.home = self.core == self.layer
        self.base = self.wide ^ jnp.where(self.home, 0, self.pair)
        self.swap_pairs = [
            (s * self.n + w, (1 - s) * self.n + (w ^ self.pair))
            for s in range(2)
            for w in range(self.n)
            if s != self.layer_of(w)
        ]

    def layer_of(self, w):
        z = w // self.quarter
        return 1 - ((z ^ (z >> 1)) & 1)

    def move(self, x, how):
        if how == "swap":
            return lax.ppermute(x, ("section", "wide"), self.swap_pairs)
        if how == "core":
            return lax.ppermute(x, "section", [(0, 1), (1, 0)])
        return lax.ppermute(x, "wide", [(w, w ^ how) for w in range(self.n)])

    def swapped(self, x):
        return jnp.where(self.home, x, self.move(x, "swap"))

    def lane_order(self, lane):
        return self.low if lane == 0 else self.low[::-1]

    def gathered_masks(self):
        own = [(self.zmask if iz else 0) ^ r for iz in range(2) for r in range(self.quarter)]
        return own + [m ^ self.pair for m in own]

    def summed_masks(self, lane):
        masks = [0]
        for bit in [self.zmask] + self.lane_order(lane)[::-1] + [self.pair]:
            masks = masks + [m ^ bit for m in masks]
        return masks


def move_many(places, arrays, how):
    flat = [a.reshape(-1, a.shape[-1]) for a in arrays]
    moved = places.move(jnp.concatenate(flat, 0) if len(flat) > 1 else flat[0], how)
    parts, at = [], 0
    for a, f in zip(arrays, flat):
        parts.append(moved[at : at + f.shape[0]].reshape(a.shape))
        at += f.shape[0]
    return parts


def run_gather(places, chunks):
    nbits = len(places.low)
    items = []
    for start, lane, rows in chunks:
        stages = ["swap", places.zmask] + places.lane_order(lane) + ["core"]
        items.append([start, stages, rows.reshape((1,) * (nbits + 1) + rows.shape)])
    results = [None] * len(items)
    tick = 0
    while any(r is None for r in results):
        groups = {}
        for i, (start, stages, arr) in enumerate(items):
            if tick >= start and stages:
                groups.setdefault(stages[0], []).append(i)
        for how, members in groups.items():
            moved = move_many(places, [items[i][2] for i in members], how)
            for i, got in zip(members, moved):
                arr = items[i][2]
                items[i][1] = items[i][1][1:]
                if how == "swap":
                    items[i][2] = jnp.where(places.home, arr, got)
                elif how == "core":
                    shape = (places.n // 2,) + arr.shape[-2:]
                    results[i] = (arr.reshape(shape), got.reshape(shape))
                else:
                    axis = 0 if how == places.zmask else 1 + nbits - 1 - places.low.index(how)
                    items[i][2] = jnp.concatenate([arr, got], axis)
        tick += 1
    return results


def run_sum(places, chunks):
    items = []
    for start, lane, blocks in chunks:
        stages = ["core"] + places.lane_order(lane) + [places.zmask]
        items.append([start, stages, blocks.reshape((2,) * len(stages) + blocks.shape[1:])])
    tick = 0
    while any(stages for _, stages, _ in items):
        groups = {}
        for i, (start, stages, arr) in enumerate(items):
            if tick >= start and stages:
                groups.setdefault(stages[0], []).append(i)
        for how, members in groups.items():
            moved = move_many(places, [items[i][2][1] for i in members], how)
            for i, got in zip(members, moved):
                items[i][1] = items[i][1][1:]
                total = items[i][2][0].astype(F32) + got.astype(F32)
                items[i][2] = total.astype(BF) if items[i][1] else total
        tick += 1
    finals = [arr for _, _, arr in items]
    moved = move_many(places, [a.astype(BF) for a in finals], "swap")
    return [jnp.where(places.home, a, m.astype(F32)) for a, m in zip(finals, moved)]


def mm(a, b):
    return jnp.dot(a, b, preferred_element_type=F32)


def mm_nt(a, b):
    return lax.dot_general(a, b, (((1,), (1,)), ((), ())), preferred_element_type=F32)


def mm_tn(a, b):
    return lax.dot_general(a, b, (((0,), (0,)), ((), ())), preferred_element_type=F32)


def relative_table(width):
    distance = (VISIBLE_KEYS - 1 - jnp.arange(VISIBLE_KEYS)).astype(F32)
    inv_freq = 1.0 / 10000.0 ** (jnp.arange(0, width, 2).astype(F32) / width)
    angles = distance[:, None] * inv_freq[None, :]
    return jnp.concatenate([jnp.sin(angles), jnp.cos(angles)], axis=1)


def statistics(rows):
    average = jnp.mean(rows, -1, keepdims=True)
    centered = rows - average
    inverse = lax.rsqrt(jnp.mean(centered * centered, -1, keepdims=True) + EPSILON)
    return centered * inverse, inverse


def norm_back(grad_hat, normed, inverse):
    first = jnp.mean(grad_hat, -1, keepdims=True)
    second = jnp.mean(grad_hat * normed, -1, keepdims=True)
    return inverse * (grad_hat - first - normed * second)


def shift_rows(table):
    h, rows, cols = table.shape
    padded = jnp.pad(table, ((0, 0), (0, 0), (0, rows))).reshape(h, -1)
    padded = padded[:, rows - 1 : rows - 1 + rows * (cols + rows - 1)]
    return padded.reshape(h, rows, cols + rows - 1)[..., :cols]


def unshift_rows(grad):
    h, rows, cols = grad.shape
    spread = jnp.pad(grad, ((0, 0), (0, 0), (0, rows - 1))).reshape(h, -1)
    return jnp.pad(spread, ((0, 0), (rows - 1, 1))).reshape(h, rows, cols + rows)[..., :cols]


def heads(x):
    return x.reshape(x.shape[0], HEADS, HEAD_WIDTH).transpose(1, 0, 2)


def unheads(x):
    return x.transpose(1, 0, 2).reshape(x.shape[1], HEADS * HEAD_WIDTH)


def bmm(pattern, a, b):
    return jnp.einsum(pattern, a, b, preferred_element_type=F32)


def layer_forward(x, memory_kv, w):
    normed, inverse = statistics(x.astype(F32))
    context = (normed * w["norm_gain"]).astype(BF)
    query = mm(context, w["q"])
    q_content = ((query + w["content_bias"]) * SCALE).astype(BF)
    q_position = ((query + w["position_bias"]) * SCALE).astype(BF)
    keys = jnp.concatenate([memory_kv[0], mm(context, w["key"]).astype(BF)], 0)
    values = jnp.concatenate([memory_kv[1], mm(context, w["value"]).astype(BF)], 0)
    scores = bmm("hid,hjd->hij", heads(q_content), heads(keys))
    scores = scores + shift_rows(bmm("hid,hpd->hip", heads(q_position), heads(w["rel"])))
    row = lax.broadcasted_iota(jnp.int32, (SEG, VISIBLE_KEYS), 0)
    col = lax.broadcasted_iota(jnp.int32, (SEG, VISIBLE_KEYS), 1)
    scores = jnp.where(col <= row + (CMEM + MEM), scores, -1e30)
    probs = jnp.exp(scores - jnp.max(scores, -1, keepdims=True))
    probs = (probs / jnp.sum(probs, -1, keepdims=True)).astype(BF)
    mixed = unheads(bmm("hij,hjd->hid", probs, heads(values)).astype(BF))
    middle = x.astype(F32) + mm(mixed, w["out"])
    mid_normed, mid_inverse = statistics(middle)
    ffn_in = (mid_normed * w["ffn_gain"]).astype(BF)
    pre = mm(ffn_in, w["up"]) + w["up_bias"]
    cdf = 0.5 * (1.0 + lax.erf(pre * 0.7071067811865476))
    hidden = (pre * cdf).astype(BF)
    slope = (cdf + pre * (jnp.exp(-0.5 * pre * pre) * 0.3989422804014327)).astype(BF)
    output = middle + mm(hidden, w["down"]) + w["down_bias"]
    saved = dict(
        normed=normed, inverse=inverse, context=context, q_content=q_content, q_position=q_position, keys=keys,
        values=values, probs=probs, mixed=mixed, mid_normed=mid_normed, mid_inverse=mid_inverse, ffn_in=ffn_in,
        hidden=hidden, slope=slope,
    )
    return output.astype(BF), saved


def layer_backward(g_low, s, w):
    g_out = g_low.astype(F32)
    g_pre = (mm_nt(g_low, w["down"]) * s["slope"].astype(F32)).astype(BF)
    g_ffn = mm_nt(g_pre, w["up"])
    g_middle = g_out + norm_back(g_ffn * w["ffn_gain"], s["mid_normed"], s["mid_inverse"])
    g_mid_low = g_middle.astype(BF)
    g_mixed = heads(mm_nt(g_mid_low, w["out"]).astype(BF))
    values, keys, probs = heads(s["values"]), heads(s["keys"]), s["probs"]
    g_probs = bmm("hid,hjd->hij", g_mixed, values)
    g_values = unheads(bmm("hij,hid->hjd", probs, g_mixed)).astype(BF)
    p = probs.astype(F32)
    g_scores = (p * (g_probs - jnp.sum(g_probs * p, -1, keepdims=True))).astype(BF)
    g_qc = unheads(bmm("hij,hjd->hid", g_scores, keys))
    g_keys = unheads(bmm("hij,hid->hjd", g_scores, heads(s["q_content"]))).astype(BF)
    g_table = unshift_rows(g_scores)
    g_qp = unheads(bmm("hip,hpd->hid", g_table, heads(w["rel"])))
    g_rel = unheads(bmm("hip,hid->hpd", g_table, heads(s["q_position"]))).astype(BF)
    g_query = ((g_qc + g_qp) * SCALE).astype(BF)
    tail = CMEM + MEM
    g_context = mm_nt(g_keys[tail:], w["key"]) + mm_nt(g_values[tail:], w["value"]) + mm_nt(g_query, w["q"])
    g_in = g_middle + norm_back(g_context * w["norm_gain"], s["normed"], s["inverse"])
    grads = dict(
        g_out=g_low, g_pre=g_pre, g_mid=g_mid_low, g_query=g_query, g_keys=g_keys, g_values=g_values, g_rel=g_rel,
        content=jnp.sum(g_qc, 0) * SCALE, position=jnp.sum(g_qp, 0) * SCALE,
    )
    return g_in, grads


def shards(
    inputs, memories, cmems, cotangent, q_weight, key_weight, value_weight, pos_weight, out_weight, up_weight,
    down_weight, comp_weight, norm_gain, content_bias, position_bias, ffn_gain, up_bias, down_bias,
):
    at = Places()
    first = at.first
    width = q_weight.shape[-1]
    ff = up_weight.shape[-1]
    rows = q_weight.shape[1]
    folds = ff // width
    n = at.n

    vectors = jnp.concatenate(
        [v[0] for v in (norm_gain, content_bias, position_bias, ffn_gain, down_bias, up_bias)]
    )
    vector_rows = 16
    vectors = jnp.pad(vectors, (0, vector_rows * width - vectors.shape[0])).reshape(vector_rows, width)
    up_pages = [up_weight[0][:, c * width : (c + 1) * width] for c in range(folds)]
    down_rows = down_weight[0]
    half = down_rows.shape[0] // 2
    comp = comp_weight[0]
    chunks = [
        (0, 0, jnp.concatenate([q_weight[0], key_weight[0]], 0)),
        (0, 1, jnp.concatenate([value_weight[0], pos_weight[0], vectors], 0)),
        (1, 0, jnp.concatenate(up_pages[:2], 0)),
        (1, 1, jnp.concatenate([down_rows[:half], out_weight[0]], 0)),
        (2, 0, jnp.concatenate(up_pages[2:], 0)),
        (2, 1, down_rows[half:]),
        (3, 0, jnp.concatenate([comp[0], comp[1]], 0)),
        (3, 1, comp[2]),
    ]
    gathered = run_gather(at, chunks)
    masks = at.gathered_masks()
    from_w = [masks.index(w) for w in range(n)]
    order = jnp.array(from_w, jnp.int32)[jnp.arange(n) ^ at.base]
    whole = [jnp.take(jnp.concatenate(halves, 0), order, axis=0) for halves in gathered]

    def matrix(chunk, start, count=1):
        return whole[chunk][:, start * rows : (start + count) * rows].reshape(n * count * rows, width)

    flat_vectors = whole[1][:, 2 * rows :].reshape(n, vector_rows * width)
    parts, start = [], 0
    for size in (rows, rows, rows, rows, rows, ff // n):
        parts.append(flat_vectors[:, start : start + size].reshape(-1).astype(F32))
        start += size
    half_blocks = [whole[c][:, :half].reshape(n, 1, half, width) for c in (3, 5)]
    w = dict(
        q=matrix(0, 0), key=matrix(0, 1), value=matrix(1, 0), out=whole[3][:, half:].reshape(width, width),
        up=jnp.concatenate([matrix(2, 0), matrix(2, 1), matrix(4, 0), matrix(4, 1)], 1),
        down=jnp.concatenate(half_blocks, 1).reshape(ff, width),
        norm_gain=parts[0], content_bias=parts[1], position_bias=parts[2], ffn_gain=parts[3], down_bias=parts[4],
        up_bias=parts[5],
    )
    table = relative_table(width).astype(BF)
    w["rel"] = mm(table, matrix(1, 1)).astype(BF)
    comp_flat = jnp.concatenate([matrix(6, 0), matrix(6, 1), matrix(7, 0)], 0)

    memory = at.swapped(jnp.stack([cmems[0][:, 0], memories[0][:, 0]], 1))
    micro = memory.shape[0]
    crossing = at.move(jnp.where(first, cotangent[:, 0], inputs[:, 0]), "swap")
    x_own = jnp.where(at.home, inputs[:, 0], crossing)
    g_own = jnp.where(at.home, cotangent[:, 0], crossing)

    memory_rows = memory.reshape(-1, width)
    memory_context = (statistics(memory_rows.astype(F32))[0] * w["norm_gain"]).astype(BF)
    memory_kv = jnp.stack([mm(memory_context, w["key"]).astype(BF), mm(memory_context, w["value"]).astype(BF)])
    memory_kv = memory_kv.reshape(2, micro, CMEM + MEM, width)
    memory_context = memory_context.reshape(micro, CMEM + MEM, width)

    oldest = memory[:, 1, : 3 * CNEW].reshape(micro * CNEW, 3 * width)
    squeezed = mm(oldest, comp_flat).astype(BF)
    g_rebuilt = ((mm_nt(squeezed, comp_flat) - oldest.astype(F32)) * (2.0 / (3 * CNEW))).astype(BF)
    g_squeezed = mm(g_rebuilt, comp_flat).astype(BF)
    g_comp = mm_tn(jnp.concatenate([g_rebuilt, oldest], 0), jnp.concatenate([squeezed, g_squeezed], 0))

    y1, s1 = layer_forward(x_own[0], memory_kv[:, 0], w)
    r1 = at.move(y1, at.pair)
    y2, s2 = layer_forward(
        jnp.where(first, x_own[1], r1), jnp.where(first, memory_kv[:, 1], memory_kv[:, 0]), w
    )
    r2 = at.move(y2, at.pair)
    y3, s3 = lax.cond(
        first, lambda: (y1, s1), lambda: layer_forward(r2, memory_kv[:, 1], w)
    )
    own_out = jnp.stack([jnp.where(first, y1, y2), jnp.where(first, y2, y3)])
    activations = at.swapped(own_out)

    g1, d1 = layer_backward(g_own[0], s2, w)
    b1 = at.move(g1.astype(BF), at.pair)
    g2, d2 = layer_backward(jnp.where(first, b1, g_own[1]), s3, w)
    b2 = at.move(g2.astype(BF), at.pair)
    g3, d3 = lax.cond(first, lambda: layer_backward(b2, s2, w), lambda: (g1, d1))
    own_grad = jnp.stack([jnp.where(first, g2, g1), jnp.where(first, g3, g2)])
    input_grads = jnp.where(at.home, own_grad, at.move(own_grad.astype(BF), "swap").astype(F32))

    def both(name, left, right):
        return jnp.concatenate([left[name], right[name]], 0)

    def saved(name):
        return both(name, s3, s2)

    def graded(name):
        return both(name, d2, d3)

    slot_memory = [jnp.where(first, memory_context[0], memory_context[1]), jnp.where(first, memory_context[1], memory_context[0])]
    context_rows = jnp.concatenate([slot_memory[0], s3["context"], slot_memory[1], s2["context"]], 0)
    g_down = mm_tn(saved("hidden"), graded("g_out")).astype(BF)
    g_up = mm_tn(saved("ffn_in"), graded("g_pre")).astype(BF)
    g_outw = mm_tn(saved("mixed"), graded("g_mid")).astype(BF)
    g_q = mm_tn(saved("context"), graded("g_query")).astype(BF)
    g_key = mm_tn(context_rows, graded("g_keys")).astype(BF)
    g_value = mm_tn(context_rows, graded("g_values")).astype(BF)
    g_rel = (d2["g_rel"].astype(F32) + d3["g_rel"].astype(F32)).astype(BF)
    g_pos = mm_tn(table, g_rel).astype(BF)
    vec = [
        d2["content"] + d3["content"],
        d2["position"] + d3["position"],
        jnp.sum(graded("g_out").astype(F32), 0),
        jnp.sum(graded("g_pre").astype(F32), 0),
    ]
    vec = jnp.concatenate([v.reshape(n, -1) for v in vec], 1).astype(BF)
    vec_size = vec.shape[1]
    vec = jnp.pad(vec, ((0, 0), (0, vector_rows * width - vec_size))).reshape(n, vector_rows, width)

    def blocks(*arrays):
        return jnp.concatenate([a.reshape(n, -1, width) for a in arrays], 1)

    def lane_blocks(lane, *arrays):
        return jnp.take(blocks(*arrays), at.base ^ jnp.array(at.summed_masks(lane), jnp.int32), axis=0)

    g_comp = g_comp.astype(BF).reshape(3, width, width)
    g_up_pages = [g_up[:, c * width : (c + 1) * width] for c in range(folds)]
    g_down_blocks = g_down.reshape(n, 2, half, width)
    summed = run_sum(
        at,
        [
            (0, 0, lane_blocks(0, g_comp[0], g_comp[1])),
            (0, 1, lane_blocks(1, g_comp[2])),
            (0, 0, lane_blocks(0, g_down_blocks[:, 0], g_up_pages[0])),
            (0, 1, lane_blocks(1, g_down_blocks[:, 1], g_up_pages[1])),
            (1, 0, lane_blocks(0, g_up_pages[2], g_outw)),
            (1, 1, lane_blocks(1, g_up_pages[3])),
            (2, 0, lane_blocks(0, g_q, g_key, vec)),
            (2, 1, lane_blocks(1, g_value, g_pos)),
        ],
    )
    s_comp = jnp.concatenate([summed[0], summed[1]], 0).reshape(3, rows, width)
    s_down = jnp.concatenate([summed[2][:half], summed[3][:half]], 0)
    s_up = jnp.concatenate([summed[2][half:], summed[3][half:], summed[4][:rows], summed[5]], 1)
    s_out = summed[4][rows:]
    s_q, s_key = summed[6][:rows], summed[6][rows : 2 * rows]
    s_value, s_pos = summed[7][:rows], summed[7][rows:]
    s_vec = summed[6][2 * rows :].reshape(-1)
    cuts, start = [], 0
    for size in (rows, rows, rows, ff // n):
        cuts.append(s_vec[start : start + size])
        start += size
    s_norm = jnp.sum(
        q_weight[0].astype(F32) * s_q + key_weight[0].astype(F32) * s_key + value_weight[0].astype(F32) * s_value, 1
    ) / norm_gain[0].astype(F32)
    s_ffn = jnp.sum(up_weight[0].astype(F32) * s_up, 1) / ffn_gain[0].astype(F32)
    outs = (
        activations[:, None], input_grads[:, None], s_q, s_key, s_value, s_pos, s_out, s_up, s_down, s_comp, s_norm,
        cuts[0], cuts[1], s_ffn, cuts[3], cuts[2],
    )
    return tuple(o[None] for o in outs)


def solution(mesh):
    rows = P("section", "wide", None)
    vector = P("section", "wide")
    stream = P("section", None, "wide", None, None)
    taps = P("section", None, "wide", None)
    whole = P(None, "wide", None, None)
    return jax.shard_map(
        shards,
        mesh=mesh,
        in_specs=(whole, stream, stream, whole) + (rows,) * 7 + (taps,) + (vector,) * 6,
        out_specs=(stream, stream) + (rows,) * 7 + (taps,) + (vector,) * 6,
        check_vma=False,
    )
```

```python
import functools

import jax
import jax.numpy as jnp
from jax import lax
from jax.experimental import pallas as pl
from jax.experimental.pallas import tpu as pltpu
from jax.sharding import PartitionSpec as P

HEADS = 8
HEAD_WIDTH = 128
MEM = 128
CMEM = 128
PAST = MEM + CMEM
SEG = 256
CNEW = 32
VISIBLE_KEYS = 512
PAGE = 512
VECTOR_ROWS = 16
STAGES = "stages"
PIECES = "pieces"
TERMS = "terms"
STEP = "step"
ITEMS = "items"
PARTS = "parts"
AUTO = "vmem"
PIN = "pin"
HBM = "hbm"
SECTION = "section"
WIDE = "wide"
G_LOW = "g_low"
SWAP = "swap"
CORE = "core"
OUT = "out"
CONTEXT = "context"
EPSILON = 1e-05
SCALE = HEAD_WIDTH ** (-0.5)
BF = jnp.bfloat16
F32 = jnp.float32
SLACK = 5 * 1024 * 1024


class Places:
    def __init__(self):
        self.n = lax.axis_size(WIDE)
        self.pair = self.n // 2
        self.bits = []
        bit = 1
        while bit < self.pair:
            self.bits.append(bit)
            bit *= 2
        self.wide = lax.axis_index(WIDE)
        self.core = lax.axis_index(SECTION)
        self.layer = self.wide // self.pair
        self.first = self.layer == 0
        self.home = self.core == self.layer
        self.base = self.wide ^ jnp.where(self.home, 0, self.pair)
        self.swap_pairs = [
            (s * self.n + w, (1 - s) * self.n + (w ^ self.pair))
            for s in range(2)
            for w in range(self.n)
            if s != w // self.pair
        ]

    def move(self, x, how):
        if how == SWAP:
            return lax.ppermute(x, (SECTION, WIDE), self.swap_pairs)
        if how == CORE:
            return lax.ppermute(x, SECTION, [(0, 1), (1, 0)])
        if how == "up":
            return lax.ppermute(x, WIDE, [(w, w + self.pair) for w in range(self.pair)])
        if how == "down":
            return lax.ppermute(x, WIDE, [(w + self.pair, w) for w in range(self.pair)])
        return lax.ppermute(x, WIDE, [(w, w ^ how) for w in range(self.n)])

    def lane_bits(self, lane):
        turn = lane * len(self.bits) // 3
        return self.bits[turn:] + self.bits[:turn]

    def summed_masks(self, lane):
        masks = [0]
        for bit in self.lane_bits(lane)[::-1] + [self.pair]:
            masks = masks + [m ^ bit for m in masks]
        return masks


def tie(values, after):
    after = [a for a in jax.tree.leaves(after)]
    return lax.optimization_barrier((values, after))[0] if after else values


def move_many(places, arrays, how):
    flat = [a.reshape(-1, a.shape[-1]) for a in arrays]
    moved = places.move(jnp.concatenate(flat, 0) if len(flat) > 1 else flat[0], how)
    parts, at = [], 0
    for a, f in zip(arrays, flat):
        parts.append(moved[at : at + f.shape[0]].reshape(a.shape))
        at += f.shape[0]
    return parts


class Gather:
    def __init__(self, places):
        self.places = places
        self.items = []
        self.flips = []
        self.last = []

    def add(self, lane, rows):
        item = dict(stages=self.places.lane_bits(lane), arr=rows[None], masks=[0], pieces=[], count=rows.shape[0])
        self.items.append(item)
        return item

    def tick(self, after=(), crossing=None, merge=True):
        at = self.places
        active = [item for item in self.items if item[STAGES]]
        tied = tie([item["arr"] for item in active], [self.last, after])
        last, groups, fresh = [], {}, []
        for item, arr in zip(active, tied):
            item["arr"] = arr
            groups.setdefault(item[STAGES][0], []).append(item)
        for how, members in groups.items():
            moved = move_many(at, [item["arr"] for item in members], how)
            last += moved
            for item, got in zip(members, moved):
                item[STAGES] = item[STAGES][1:]
                arr, masks = item["arr"], item["masks"]
                other = [m ^ how for m in masks]
                if item[STAGES]:
                    item["arr"], item["masks"] = jnp.concatenate([arr, got], 0), masks + other
                else:
                    self.flips.append((item, arr, masks))
                    fresh.append((item, got, other))
        count = len(self.flips) if crossing is None else crossing
        now, self.flips = self.flips[:count], self.flips[count:] + fresh
        flat = [arr.reshape(-1, PAGE) for _, arr, _ in now]
        if merge and now:
            got = at.move(tie(jnp.concatenate(flat, 0), [self.last, after]), CORE)
            last.append(got)
            ends = [sum(f.shape[0] for f in flat[:i]) for i in range(len(flat) + 1)]
            gots = [got[a:b] for a, b in zip(ends, ends[1:])]
        else:
            gots = []
            for f in flat:
                gots.append(at.move(tie(f, [self.last, after]), CORE))
            last += gots
        for (item, _, masks), arr, got in zip(now, flat, gots):
            item[PIECES] += [(arr, masks), (got, [m ^ at.pair for m in masks])]
        self.last = last
        return last

    def until(self, items, merge=True):
        while any(len(item[PIECES]) < 4 for item in items):
            self.tick(merge=merge)


class Sum:
    def __init__(self, places):
        self.places = places
        self.groups = []

    def add(self, heights, *parts):
        items = [dict(stages=self.places.lane_bits(lane), terms=[], out=None) for lane in range(len(heights))]
        group = dict(heights=heights, parts=parts, step=0, items=items)
        self.groups.append(group)
        return group

    def lanes(self, group, flat):
        quarter, parts, at = self.places.n // 4, [], 0
        for height in group["heights"]:
            parts.append(flat[at : at + quarter * height].reshape(quarter, height, PAGE))
            at += quarter * height
        return parts

    def total(self, terms, dtype):
        return sum(t.astype(F32) for t in terms).astype(dtype)

    def tick(self, groups, after=()):
        at = self.places
        going = [(group, item) for group in groups if group[STEP] > 0 for item in group[ITEMS] if item[STAGES]]
        crossing = [group for group in groups if group[STEP] == 0 or (group[STEP] == 1 and len(group[PARTS]) == 4)]
        operands = []
        for group, item in going:
            if group[STEP] == 1:
                operands.append(item["half"])
            else:
                half = item[TERMS][0].shape[0] // 2
                operands.append(self.total([t[half:] for t in item[TERMS]], BF))
                item[TERMS] = [t[:half] for t in item[TERMS]]
        sends = [group[PARTS][-1 - group[STEP]] for group in crossing]
        operands = tie(operands + sends, after)
        last, ways = [], {}
        for (group, item), operand in zip(going, operands):
            ways.setdefault(item[STAGES][0], []).append((item, operand))
        for how, members in ways.items():
            moved = move_many(at, [operand for _, operand in members], how)
            last += moved
            for (item, _), got in zip(members, moved):
                item[STAGES] = item[STAGES][1:]
                item[TERMS].append(got)
        for group, operand in zip(crossing, operands[len(going) :]):
            got = at.move(operand, CORE)
            last.append(got)
            if len(group[PARTS]) == 2:
                rows = got.shape[0] // 2
                pairs = [(group[PARTS][0][:rows], got[:rows]), (group[PARTS][0][rows:], got[rows:])]
            else:
                pairs = [None, None]
                pairs[1 - group[STEP]] = (group[PARTS][1 - group[STEP]], got)
            if pairs[0]:
                for item, a, b in zip(group[ITEMS], *[self.lanes(group, p) for p in pairs[0]]):
                    item[TERMS] += [a, b]
            if pairs[1]:
                for item, a, b in zip(group[ITEMS], *[self.lanes(group, p) for p in pairs[1]]):
                    item["half"] = self.total([a, b], BF)
        for group in groups:
            group[STEP] += 1
        return last

    def finish(self, groups, after=()):
        at = self.places
        items = [item for group in groups for item in group[ITEMS]]
        while any(item[STAGES] for item in items):
            self.tick([group for group in groups if any(item[STAGES] for item in group[ITEMS])])
        finals = [self.total(item[TERMS], F32)[0] for item in items]
        moved = move_many(at, tie([a.astype(BF) for a in finals], after), SWAP)
        for item, a, got in zip(items, finals, moved):
            item[OUT] = jnp.where(at.home, a, got.astype(F32))
        return moved


def mm(a, b):
    return jnp.dot(a, b, preferred_element_type=F32)


def mm_nt(a, b):
    return lax.dot_general(a, b, (((1,), (1,)), ((), ())), preferred_element_type=F32)


def mm_tn(a, b):
    return lax.dot_general(a, b, (((0,), (0,)), ((), ())), preferred_element_type=F32)


def statistics(rows):
    average = jnp.mean(rows, -1, keepdims=True)
    centered = rows - average
    inverse = lax.rsqrt(jnp.mean(centered * centered, -1, keepdims=True) + EPSILON)
    return centered * inverse, inverse


def norm_back(grad_hat, normed, inverse):
    first = jnp.mean(grad_hat, -1, keepdims=True)
    second = jnp.mean(grad_hat * normed, -1, keepdims=True)
    return inverse * (grad_hat - first - normed * second)


def relative_table(inv_freq, reverse):
    step = jnp.arange(VISIBLE_KEYS) if reverse else VISIBLE_KEYS - 1 - jnp.arange(VISIBLE_KEYS)
    angles = step.astype(F32)[:, None] * inv_freq[None, :]
    return jnp.concatenate([jnp.sin(angles), jnp.cos(angles)], axis=1).astype(BF)


def columns(at):
    return slice(at * PAGE, (at + 1) * PAGE)


class Copies:
    def __init__(self, sems):
        self.sems = sems
        self.used = 0
        self.open = []

    def start(self, source, target):
        copy = pltpu.make_async_copy(source, target, self.sems.at[self.used])
        copy.start()
        self.used += 1
        self.open.append(copy)
        return copy

    def wait(self, copies=None):
        for copy in self.open[:] if copies is None else copies:
            copy.wait()
            self.open.remove(copy)


def pack_kernel(first_ref, *refs):
    (q, key, value, pos, out, up, down, comp, cmems, memories, inputs, cotangent, vectors) = refs[:13]
    pack_a, pack_b, pack_s, pack_t = refs[13:17]
    copies = Copies(refs[17])
    rows, fold = q.shape[0], down.shape[0]

    def put(target, at, source, count):
        for c in range(source.shape[-1] // PAGE):
            copies.start(source.at[:, columns(c)], target.at[pl.ds(at, count)])
            at += count
        return at

    def either(target, row):
        sem = copies.sems.at[copies.used]
        copies.used += 1

        @pl.when(first_ref[0] == 1)
        def _():
            pltpu.make_async_copy(cotangent.at[row], target, sem).start()

        @pl.when(first_ref[0] == 0)
        def _():
            pltpu.make_async_copy(inputs.at[row], target, sem).start()

        copies.open.append(pltpu.make_async_copy(inputs.at[row], target, sem))

    at = put(pack_a, 0, q, rows) + VECTOR_ROWS
    for source in (key, value):
        at = put(pack_a, at, source, rows)
    put(pack_a, at, pos, rows)
    at = put(pack_b, 0, up, rows)
    at = put(pack_b, at, down, fold)
    put(pack_b, at, out, rows)
    at = 0
    for i in range(memories.shape[0]):
        for source in (cmems, memories):
            copies.start(source.at[i], pack_s.at[pl.ds(at, source.shape[1])])
            at += source.shape[1]
    either(pack_s.at[pl.ds(at, SEG)], 0)
    at = 0
    for i in range(1, inputs.shape[0]):
        either(pack_t.at[pl.ds(at, SEG)], i)
        at += SEG
    for t in range(3):
        copies.start(comp.at[t], pack_t.at[pl.ds(at, rows)])
        at += rows
    start = q.shape[1] // PAGE * rows
    pack_a[start : start + VECTOR_ROWS, :] = vectors[...].astype(BF)
    copies.wait()


def put_blocks(base, source, count, masks, first, rows, target, column):
    for i, mask in enumerate(masks):
        at = pl.multiple_of((base ^ mask) * rows, rows)
        target[pl.ds(at, rows), column : column + PAGE] = source[i * count + first : i * count + first + rows, :]


def assemble_kernel(items, base_ref, *refs):
    base = base_ref[0]
    sources = sum(len(masks) for masks, _, _ in items)
    at = 0
    for masks, count, parts in items:
        for first, rows, out, column in parts:
            for i, blocks in enumerate(masks):
                put_blocks(base, refs[at + i], count, blocks, first, rows, refs[sources + out], column)
        at += len(masks)


def prepare_kernel(memory, vecs, table, table_rev, key, value, pos0, pos1, context0, context1, kmem0, vmem0, kmem1, vmem1, rel,
                   rel_rev, ctx, sems):
    copies = Copies(sems)
    ctx[...] = (statistics(memory[...].astype(F32))[0] * vecs[0:1, :]).astype(BF)
    for h, context in enumerate((context0, context1)):
        copies.start(ctx.at[pl.ds(h * PAST, PAST)], context)
    for h in range(2):
        rows = slice(h * PAST, (h + 1) * PAST)
        (kmem0, kmem1)[h][...] = mm(ctx[rows, :], key[...]).astype(BF)
        (vmem0, vmem1)[h][...] = mm(ctx[rows, :], value[...]).astype(BF)
    for c, pos in enumerate((pos0, pos1)):
        rel[:, columns(c)] = mm(table[...], pos[...]).astype(BF)
        rel_rev[:, columns(c)] = mm(table_rev[...], pos[...]).astype(BF)
    copies.wait()


def forward_attention_kernel(x, kmem, vmem, rel, vecs, q, key, value, context, q_content, q_position, kx, vx, probs,
                             mixed, ctx, sems):
    copies = Copies(sems)
    ctx[...] = (statistics(x[...].astype(F32))[0] * vecs[0:1, :]).astype(BF)
    copies.start(ctx, context)
    for h in range(2):
        query = mm(ctx[...], q[:, columns(h)])
        q_content[:, columns(h)] = ((query + vecs[1:2, columns(h)]) * SCALE).astype(BF)
        q_position[:, columns(h)] = ((query + vecs[2:3, columns(h)]) * SCALE).astype(BF)
        kx[:, columns(h)] = mm(ctx[...], key[:, columns(h)]).astype(BF)
        vx[:, columns(h)] = mm(ctx[...], value[:, columns(h)]).astype(BF)
    row = lax.broadcasted_iota(jnp.int32, (SEG, VISIBLE_KEYS), 0)
    col = lax.broadcasted_iota(jnp.int32, (SEG, VISIBLE_KEYS), 1)
    allowed = col <= row + PAST
    for h in range(HEADS):
        hs = slice(h * HEAD_WIDTH, (h + 1) * HEAD_WIDTH)
        qc, qp = q_content[:, hs], q_position[:, hs]
        scores = jnp.concatenate([mm_nt(qc, kmem[:, hs]), mm_nt(qc, kx[:, hs])], 1)
        position = pltpu.roll(mm_nt(qp, rel[:, hs]), VISIBLE_KEYS - SEG + 1, 1, stride=1, stride_axis=0)
        scores = jnp.where(allowed, scores + position, -1e30)
        weight = jnp.exp(scores - jnp.max(scores, -1, keepdims=True))
        low = (weight * (1.0 / jnp.sum(weight, -1, keepdims=True))).astype(BF)
        probs[h] = low
        mixed[:, hs] = (mm(low[:, :PAST], vmem[:, hs]) + mm(low[:, PAST:], vx[:, hs])).astype(BF)
    copies.wait()


def forward_ffn_kernel(keep, x, mixed, vecs, up_bias, out, up0, up1, down0, down1, y, *refs):
    if keep:
        normed2, inverse2, ffn_in, hidden, slope, middle, inner, acts, sems = refs
        copies = Copies(sems)
    else:
        middle, inner, acts = refs
    for h in range(2):
        middle[:, columns(h)] = x[:, columns(h)].astype(F32) + mm(mixed[...], out[:, columns(h)])
    normed, inverse = statistics(middle[...])
    inner[...] = (normed * vecs[3:4, :]).astype(BF)
    if keep:
        normed2[...] = normed
        inverse2[...] = jnp.broadcast_to(inverse, inverse2.shape)
        copies.start(inner, ffn_in)
    left = up0.shape[1] // PAGE

    def expand(source, here, there):
        pre = mm(inner[...], source[:, here]) + up_bias[0:1, there]
        cdf = 0.5 * (1.0 + lax.erf(pre * 0.7071067811865476))
        acts[:, there] = (pre * cdf).astype(BF)
        if keep:
            slope[:, there] = (cdf + pre * (jnp.exp(-0.5 * pre * pre) * 0.3989422804014327)).astype(BF)

    if keep:
        for c in range(acts.shape[1] // PAGE):
            expand(*((up0, columns(c)) if c < left else (up1, columns(c - left))), columns(c))
    else:
        for source, first in ((up0, 0), (up1, left)):

            def body(c, carry, source=source, first=first):
                here = pl.ds(pl.multiple_of(c * PAGE, PAGE), PAGE)
                expand(source, here, pl.ds(pl.multiple_of((first + c) * PAGE, PAGE), PAGE))
                return carry

            lax.fori_loop(0, source.shape[1] // PAGE, body, 0)
    if keep:
        copies.start(acts, hidden)
    for h, down in enumerate((down0, down1)):
        y[:, columns(h)] = (middle[:, columns(h)] + mm(acts[...], down[...]) + vecs[4:5, columns(h)]).astype(BF)
    if keep:
        copies.wait()


def backward_ffn_kernel(g, slope, normed2, inverse2, vecs, out, up0, up1, down0, down1, g_pre, g_mid, g_mid_low,
                        g_mixed, sums, pre, low, sems):
    copies = Copies(sems)
    sums[...] = jnp.zeros_like(sums)
    for c in range(slope.shape[1] // PAGE):
        g_hidden = mm_nt(g[:, columns(0)], down0[columns(c), :]) + mm_nt(g[:, columns(1)], down1[columns(c), :])
        g_low = (g_hidden * slope[:, columns(c)].astype(F32)).astype(BF)
        pre[:, columns(c)] = g_low
        sums[0:1, columns(c)] = jnp.sum(g_low.astype(F32), 0, keepdims=True)
    copies.start(pre, g_pre)
    g_out = g[...].astype(F32)
    sums[1:2, : g.shape[1]] = jnp.sum(g_out, 0, keepdims=True)
    half = up0.shape[1]
    g_ffn = mm_nt(pre[:, :half], up0[...]) + mm_nt(pre[:, half:], up1[...])
    g_middle = g_out + norm_back(g_ffn * vecs[3:4, :], normed2[...], inverse2[:, 0:1])
    g_mid[...] = g_middle
    low[...] = g_middle.astype(BF)
    copies.start(low, g_mid_low)
    g_mixed[...] = mm_nt(low[...], out[...]).astype(BF)
    copies.wait()


def backward_attention_kernel(g_mixed, g_mid, x, q_content, q_position, kmem, kx, vmem, vx, probs, rel_rev, vecs, q,
                              key, value, g_in, g_low, g_query, g_keys, g_values, g_rel, sums, total, query, keys,
                              values, rels, sems):
    copies = Copies(sems)
    row = lax.broadcasted_iota(jnp.int32, (VISIBLE_KEYS, VISIBLE_KEYS), 0)
    col = lax.broadcasted_iota(jnp.int32, (VISIBLE_KEYS, VISIBLE_KEYS), 1)
    flip = jnp.where(row + col == VISIBLE_KEYS - 1, 1.0, 0.0).astype(BF)
    sums[...] = jnp.zeros_like(sums)
    for h in range(HEADS):
        hs = slice(h * HEAD_WIDTH, (h + 1) * HEAD_WIDTH)
        gm, low = g_mixed[:, hs], probs[h]
        g_probs = jnp.concatenate([mm_nt(gm, vmem[:, hs]), mm_nt(gm, vx[:, hs])], 1)
        values[:, hs] = mm_tn(low, gm).astype(BF)
        p = low.astype(F32)
        g_scores = (p * (g_probs - jnp.sum(g_probs * p, -1, keepdims=True))).astype(BF)
        keys[:, hs] = mm_tn(g_scores, q_content[:, hs]).astype(BF)
        g_qc = mm(g_scores[:, :PAST], kmem[:, hs]) + mm(g_scores[:, PAST:], kx[:, hs])
        turned = pltpu.roll(mm(g_scores, flip), VISIBLE_KEYS - SEG + 1, 1, stride=1, stride_axis=0).astype(BF)
        g_qp = mm(turned, rel_rev[:, hs])
        rels[:, hs] = mm_tn(turned, q_position[:, hs]).astype(BF)
        sums[0:1, hs] = jnp.sum(g_qc, 0, keepdims=True) * SCALE
        sums[1:2, hs] = jnp.sum(g_qp, 0, keepdims=True) * SCALE
        query[:, hs] = ((g_qc + g_qp) * SCALE).astype(BF)
    for source, target in ((query, g_query), (keys, g_keys), (values, g_values), (rels, g_rel)):
        copies.start(source, target)
    g_context = mm_nt(query[...], q[...]) + mm_nt(keys[PAST:, :], key[...]) + mm_nt(values[PAST:, :], value[...])
    normed, inverse = statistics(x[...].astype(F32))
    g_x = g_mid[...] + norm_back(g_context * vecs[0:1, :], normed, inverse)
    total[...] = g_x
    copies.start(total, g_in)
    g_low[...] = g_x.astype(BF)
    copies.wait()


def views_of(outs):
    if len(outs) == 4:
        return [(out, 0) for out in outs]
    return [(out, half * (out.shape[0] // 2)) for out in outs for half in range(2)]


def scatter_blocks(base, masks, source, outs, start, height, first, rows, cut, at):
    quarter = len(masks) // 4
    for j, mask in enumerate(masks):
        where = pl.multiple_of((base ^ mask) * rows + first, 16)
        out, origin = views_of(outs)[j // quarter]
        row = origin + start + (j % quarter) * height + at
        out[row : row + cut, :] = source[pl.ds(where, cut), :]


def weight_kernel(loads, parts, vector_place, masks, heights, count, shapes, made, base_ref, *refs):
    base = base_ref[0]
    n, quarter = len(masks[0]), len(masks[0]) // 4
    ins, outs = refs[:count], refs[count : count + made]
    stacks = refs[count + made : count + made + len(shapes)]
    scratch = refs[count + made + len(shapes)]
    copies = Copies(refs[-1])
    starts = [quarter * sum(heights[:lane]) for lane in range(len(masks))]
    waiting = {}
    for number, stack, first in loads:
        target = stacks[stack].at[pl.ds(first, ins[number].shape[0])]
        waiting.setdefault(stack, []).append(copies.start(ins[number], target))
    if vector_place is not None:
        lane, at, sources = vector_place
        vector = refs[-2]
        vector[...] = jnp.zeros_like(vector)
        for i, (numbers, row) in enumerate(sources):
            total = ins[numbers[0]][row : row + 1, :] + ins[numbers[1]][row : row + 1, :]
            size = (total.shape[1] if i == 3 else shapes[0][1]) // n
            for w in range(n):
                vector[w, i : i + 1, :size] = total[:, w * size : (w + 1) * size]
        for j, mask in enumerate(masks[lane]):
            out, origin = views_of(outs)[j // quarter]
            to = origin + starts[lane] + (j % quarter) * heights[lane] + at
            out[to : to + VECTOR_ROWS, :] = vector[base ^ mask].astype(BF)
    for left, right, column, rows, spots in parts:
        for stack in (left, right):
            copies.wait(waiting.pop(stack, []))
        chunk = 1024
        for start in range(0, n * rows, chunk):
            product = mm_tn(stacks[left][:, start : start + chunk], stacks[right][:, column : column + PAGE])
            scratch[start : start + chunk, :] = product.astype(BF)
        for lane, first, cut, at in spots:
            scatter_blocks(base, masks[lane], scratch, outs, starts[lane], heights[lane], first, rows, cut, at)


def compression_kernel(masks, pieces, count, streams, base_ref, *refs):
    base = base_ref[0]
    sources = sum(len(blocks) for blocks in pieces)
    rows_of, ins, outs = refs[:streams], refs[streams : streams + sources], refs[streams + sources : streams + sources + 2]
    weight, scratch = refs[streams + sources + 2 :]
    width = weight.shape[0]
    n = len(masks[0])
    rows = width // n
    old = [[], [], []]
    row = lax.broadcasted_iota(jnp.int32, (CNEW, MEM), 0)
    col = lax.broadcasted_iota(jnp.int32, (CNEW, MEM), 1)
    for ref in rows_of:
        for t in range(3):
            pick = jnp.where(col == 3 * row + t, 1.0, 0.0).astype(BF)
            old[t].append(mm(pick, ref[CMEM:, :]).astype(BF))
    old = [jnp.concatenate(o, 0) for o in old]

    def load(t):
        at = sum(len(blocks) for blocks in pieces[:t])
        for i, blocks in enumerate(pieces[t]):
            for h in range(width // PAGE):
                put_blocks(base, ins[at + i], count, blocks, h * rows, rows, weight, h * PAGE)

    squeezed = jnp.zeros(old[0].shape, F32)
    for t in range(3):
        load(t)
        squeezed = squeezed + mm(old[t], weight[...])
    squeezed = squeezed.astype(BF)
    g_rebuilt, g_squeezed = [], jnp.zeros(old[0].shape, F32)
    for t in range(3):
        load(t)
        rebuilt = mm_nt(squeezed, weight[...])
        g_rebuilt.append(((rebuilt - old[t].astype(F32)) * (2.0 / (3 * CNEW))).astype(BF))
        g_squeezed = g_squeezed + mm(g_rebuilt[t], weight[...])
    right = jnp.concatenate([squeezed, g_squeezed.astype(BF)], 0)
    height = width // PAGE * rows
    for t in range(3):
        left = jnp.concatenate([g_rebuilt[t], old[t]], 0)
        for h in range(width // PAGE):
            scratch[...] = mm_tn(left, right[:, columns(h)]).astype(BF)
            scatter_blocks(base, masks[t], scratch, outs, t * (n // 4) * height, height, 0, rows, rows, h * rows)


def size_of(shape, dtype):
    total = jnp.dtype(dtype).itemsize
    for s in shape:
        total *= s
    return total


def call(kernel, name, arrays, outs, scratch=(), copies=0, base=None, slack=SLACK):
    held = sum(size_of(a.shape, a.dtype) for a, place in arrays if place == AUTO)
    held += sum(size_of(s, d) for s, d, place in outs if place == AUTO) + sum(size_of(*s) for s in scratch)
    specs = dict(vmem=pltpu.VMEM, pin=pltpu.VMEM, hbm=pltpu.HBM)
    shapes = dict(vmem=jax.ShapeDtypeStruct, pin=pltpu.VMEM, hbm=pltpu.HBM)

    def placed(a, place):
        return a if place == AUTO else pltpu.with_memory_space_constraint(a, specs[place])

    scalars = [] if base is None else [base]
    return pl.pallas_call(
        kernel,
        out_shape=[shapes[place](s, d) for s, d, place in outs],
        in_specs=[pl.BlockSpec(memory_space=pltpu.SMEM)] * len(scalars)
        + [pl.BlockSpec(memory_space=specs[place]) for _, place in arrays],
        out_specs=[pl.BlockSpec(memory_space=specs[place]) for _, _, place in outs],
        scratch_shapes=[pltpu.VMEM(*s) for s in scratch] + ([pltpu.SemaphoreType.DMA((copies,))] if copies else []),
        compiler_params=pltpu.CompilerParams(vmem_limit_bytes=held + slack),
        cost_estimate=pl.CostEstimate(flops=2 * 10**9, bytes_accessed=4 * 10**6, transcendentals=0),
        name=name,
    )(*scalars, *[placed(a, place) for a, place in arrays])


def places(kind, *arrays):
    return [(a, kind) for a in arrays]


def forward_attention(x, kmem, vmem, w):
    seg = (SEG, x.shape[1])
    got = call(
        forward_attention_kernel, "forward_attention",
        places(AUTO, x) + places(PIN, kmem, vmem, w["rel"], w["vecs"], w["q"], w["key"], w["value"]),
        [(seg, BF, HBM)] + [(seg, BF, PIN)] * 4 + [((HEADS, SEG, VISIBLE_KEYS), BF, PIN), (seg, BF, PIN)],
        [(seg, BF)], 1,
    )
    return dict(zip((CONTEXT, "q_content", "q_position", "kx", "vx", "probs", "mixed"), got))


def forward_ffn(x, s, w, keep=True):
    seg, wide = (SEG, x.shape[1]), (SEG, w["up_bias"].shape[1])
    outs = [(seg, BF, AUTO)]
    if keep:
        outs += [(seg, F32, PIN), ((SEG, 128), F32, PIN), (seg, BF, HBM), (wide, BF, HBM), (wide, BF, PIN)]
    got = call(
        functools.partial(forward_ffn_kernel, keep), "forward_ffn",
        places(AUTO, x)
        + places(PIN, s["mixed"], w["vecs"], w["up_bias"], w[OUT], w["up0"], w["up1"], w["down0"], w["down1"]),
        outs, [(seg, F32), (seg, BF), (wide, BF)], 2 if keep else 0,
    )
    return got[0], dict(s, **dict(zip(("normed2", "inverse2", "ffn_in", "hidden", "slope"), got[1:])))


def backward_ffn(g, s, w):
    seg, wide = g.shape, s["slope"].shape
    got = call(
        backward_ffn_kernel, "backward_ffn",
        places(AUTO, g)
        + places(PIN, s["slope"], s["normed2"], s["inverse2"], w["vecs"], w[OUT], w["up0"], w["up1"], w["down0"],
                 w["down1"]),
        [(wide, BF, HBM), (seg, F32, PIN), (seg, BF, HBM), (seg, BF, PIN), ((8, wide[1]), F32, AUTO)],
        [(wide, BF), (seg, BF)], 2,
    )
    return dict(zip(("g_pre", "g_mid", "g_mid_low", "g_mixed", "ffn_sums"), got))


def backward_attention(d, x, kmem, vmem, s, w):
    seg, keys = x.shape, (VISIBLE_KEYS, x.shape[1])
    got = call(
        backward_attention_kernel, "backward_attention",
        places(PIN, d["g_mixed"], d["g_mid"]) + places(AUTO, x)
        + places(PIN, s["q_content"], s["q_position"], kmem, s["kx"], vmem, s["vx"], s["probs"], w["rel_rev"],
                 w["vecs"], w["q"], w["key"], w["value"]),
        [(seg, F32, HBM), (seg, BF, AUTO), (seg, BF, HBM), (keys, BF, HBM), (keys, BF, HBM), (keys, BF, HBM),
         ((8, seg[1]), F32, AUTO)],
        [(seg, F32), (seg, BF), (keys, BF), (keys, BF), (keys, BF)], 5,
    )
    return dict(zip(("g_in", G_LOW, "g_query", "g_keys", "g_values", "g_rel", "sums"), got))


def weight_grads(base, masks, name, stacks, parts, vectors=None, extra=(), joined=False):
    n = len(masks[0])
    heights = [0] * len(masks)
    for part in parts:
        for lane, _, rows, at in part[-1]:
            heights[lane] = max(heights[lane], at + rows)
    place = None
    if vectors is not None:
        place = (vectors[0], heights[vectors[0]], vectors[1])
        heights[vectors[0]] += VECTOR_ROWS
    arrays, loads, shapes = places(AUTO, *extra), [], []
    for i, stack in enumerate(stacks):
        at = 0
        for a in stack:
            loads.append((len(arrays), i, at))
            arrays.append((a, HBM))
            at += a.shape[0]
        shapes.append((at, stack[0].shape[1]))
    tallest = max([n * p[3] for p in parts])
    scratch = [(s, BF) for s in shapes] + [((tallest, PAGE), BF)]
    if vectors is not None:
        scratch.append(((n, VECTOR_ROWS, PAGE), F32))
    got = call(
        functools.partial(weight_kernel, loads, parts, place, masks, heights, len(arrays), shapes, 2 if joined else 4),
        name, arrays, [((n // (2 if joined else 4) * sum(heights), PAGE), BF, PIN)] * (2 if joined else 4), scratch, len(loads), base, 2 * SLACK,
    )
    return heights, got


def pieces_of(items):
    return [piece for item in items for piece, _ in item[PIECES]], [[m for _, m in item[PIECES]] for item in items]


def assemble(base, name, items, parts, shapes):
    arrays, masks = pieces_of(items)
    plan = [(m, item["count"], p) for m, item, p in zip(masks, items, parts)]
    return call(
        functools.partial(assemble_kernel, plan), name, places(AUTO, *arrays), [(s, BF, PIN) for s in shapes],
        base=base,
    )


def shards(
    inputs, memories, cmems, cotangent, q_weight, key_weight, value_weight, pos_weight, out_weight, up_weight,
    down_weight, comp_weight, norm_gain, content_bias, position_bias, ffn_gain, up_bias, down_bias,
):
    at = Places()
    first = at.first
    width = q_weight.shape[-1]
    ff = up_weight.shape[-1]
    rows = q_weight.shape[1]
    n = at.n
    fold = ff // n
    per, pages = width // PAGE, ff // PAGE
    base = at.base.reshape(1).astype(jnp.int32)
    masks = [at.summed_masks(lane) for lane in range(3)]
    square = per * rows
    seam = 3 * pages // 4

    micro = memories.shape[1]
    kept = micro * PAST
    sizes = [
        (4 * square + VECTOR_ROWS, PAGE), (pages * rows + per * fold + square, PAGE), (kept + SEG, width),
        ((micro - 1) * SEG + 3 * rows, width),
    ]
    vectors = [
        jnp.pad(v.astype(F32), ((0, 0), (0, PAGE - v.shape[1])))
        for v in (norm_gain, content_bias, position_bias, ffn_gain, down_bias, up_bias)
    ]
    vectors = jnp.pad(jnp.concatenate(vectors, 0), ((0, VECTOR_ROWS - len(vectors)), (0, 0)))
    pack_a, pack_b, pack_s, pack_t = call(
        pack_kernel, "pack",
        places(HBM, q_weight[0], key_weight[0], value_weight[0], pos_weight[0], out_weight[0], up_weight[0],
               down_weight[0], comp_weight[0], cmems[0, :, 0], memories[0, :, 0], inputs[:, 0], cotangent[:, 0])
        + places(AUTO, vectors),
        [(size, BF, AUTO) for size in sizes], (), 5 * per + pages + per + 3 * micro + 3,
        jnp.where(first, 1, 0).reshape(1).astype(jnp.int32),
    )

    def swapped(x, after):
        x = tie(x, after)
        got = at.move(x, SWAP)
        return jnp.where(at.home, x, got), got

    def slot(a, b):
        return jnp.where(first, a, b)

    gather = Gather(at)
    pack_a, got_a = swapped(pack_a, [])
    cuts = [square + VECTOR_ROWS, 2 * square + VECTOR_ROWS, 3 * square + VECTOR_ROWS]
    pos_rows = pack_a[cuts[2] :]
    a0 = gather.add(0, pack_a[: cuts[0]])
    a1 = gather.add(1, jnp.concatenate([pack_a[cuts[0] : cuts[1]], pos_rows[:rows]], 0))
    a2 = gather.add(2, jnp.concatenate([pack_a[cuts[1] : cuts[2]], pos_rows[rows:]], 0))
    pack_b, got_b = swapped(pack_b, [got_a])
    while len(a0[STAGES]) > 1:
        gather.tick()
    moved = gather.tick()
    pack_s = tie(pack_s, [got_b, moved])
    got_s = at.move(pack_s, SWAP)
    memory = [jnp.where(at.home, pack_s[s], got_s[s]) for s in [slice(i * PAST, (i + 1) * PAST) for i in range(micro)]]
    x_own = [jnp.where(at.home, inputs[0, 0], got_s[kept:])]
    g_own = [jnp.where(at.home, cotangent[0, 0], got_s[kept:])]
    b2 = gather.add(2, pack_b[: seam * rows])
    b1 = gather.add(1, pack_b[seam * rows : pages * rows + fold])
    b0 = gather.add(0, pack_b[pages * rows + fold :])
    gather.tick()
    while len(b0[STAGES]) > 1:
        moved = gather.tick()
    pack_t = tie(pack_t, [got_s])
    got_t = at.move(pack_t, SWAP)
    x_own.append(jnp.where(at.home, inputs[1, 0], got_t[:SEG]))
    g_own.append(jnp.where(at.home, cotangent[1, 0], got_t[:SEG]))
    comp = jnp.where(at.home, pack_t[SEG:], got_t[SEG:])

    gather.until([a0, a1, a2])
    whole = (width, width)
    w = {}
    spread = [(c * rows, rows, 0, c * PAGE) for c in range(per)]

    def spread_to(out):
        return [(c * rows, rows, out, c * PAGE) for c in range(per)]

    w["q"], w["key"], w["value"], pos0, pos1 = assemble(
        base, "assemble_attention", [a0, a1, a2],
        [spread_to(0), spread_to(1) + [(square, rows, 3, 0)], spread_to(2) + [(square, rows, 4, 0)]],
        [whole] * 3 + [(width, PAGE)] * 2,
    )
    all_masks = [m for _, ms in a0[PIECES] for m in ms]
    order = jnp.array([all_masks.index(m) for m in range(n)], jnp.int32)[jnp.arange(n) ^ at.base]
    flat = [piece.reshape(len(ms), a0["count"], PAGE)[:, square:] for piece, ms in a0[PIECES]]
    flat = jnp.take(jnp.concatenate(flat, 0), order, axis=0).astype(F32)
    w["vecs"] = flat[:, :8, :rows].transpose(1, 0, 2).reshape(8, width)
    w["up_bias"] = flat[:, 5, :fold].reshape(1, ff)
    inv_freq = tie(1.0 / 10000.0 ** (jnp.arange(0, width, 2).astype(F32) / width), [moved])
    table, table_rev = relative_table(inv_freq, False), relative_table(inv_freq, True)
    past, keys, mem = (micro * PAST, width), (VISIBLE_KEYS, width), (PAST, width)
    slots = jnp.concatenate([slot(memory[0], memory[1]), slot(memory[1], memory[0])], 0)
    ma, mb, ka, va, kb, vb, w["rel"], w["rel_rev"] = call(
        prepare_kernel, "prepare",
        places(AUTO, slots, w["vecs"], table, table_rev) + places(PIN, w["key"], w["value"], pos0, pos1),
        [(mem, BF, HBM)] * 2 + [(mem, BF, PIN)] * 4 + [(keys, BF, PIN)] * 2, [(past, BF)], 2,
    )
    s1 = forward_attention(x_own[0], ka, va, w)
    gather.tick(crossing=1, merge=False)
    gather.tick([s1["mixed"]], merge=False)
    gather.until([b0, b1, b2])
    w["up0"], w["up1"], w["down0"], w["down1"], w[OUT] = assemble(
        base, "assemble_ffn", [b2, b1, b0],
        [
            [(c * rows, rows, 0, c * PAGE) for c in range(seam)],
            [(c * rows, rows, 1, c * PAGE) for c in range(pages - seam)] + [((pages - seam) * rows, fold, 2, 0)],
            [(0, fold, 3, 0)] + [(fold + c * rows, rows, 4, c * PAGE) for c in range(per)],
        ],
        [(width, seam * PAGE), (width, (pages - seam) * PAGE), (ff, PAGE), (ff, PAGE), whole],
    )

    y1, _ = forward_ffn(x_own[0], s1, w, False)
    r1 = at.move(y1, "up")
    x2 = slot(x_own[1], r1)
    y2, s2 = forward_ffn(x2, forward_attention(x2, kb, vb, w), w)
    r2 = at.move(y2, "up")

    d1 = dict(backward_ffn(g_own[0], s2, w), g_out=g_own[0])
    d1.update(backward_attention(d1, x2, kb, vb, s2, w))
    r3 = at.move(d1[G_LOW], "down")
    x3 = tie(slot(x_own[0], r2), [d1[G_LOW]])
    y3, s3 = forward_ffn(x3, forward_attention(x3, ka, va, w), w)
    g3 = tie(slot(r3, g_own[1]), [y3])
    d2 = dict(backward_ffn(g3, s3, w), g_out=g3)
    d2.update(backward_attention(d2, x3, ka, va, s3, w))
    r4 = at.move(d2[G_LOW], "down")

    c0, c1, c2 = [
        gather.add(t, jnp.concatenate([comp[t * rows : (t + 1) * rows, columns(c)] for c in range(per)], 0))
        for t in range(3)
    ]
    gather.last = []
    gather.tick([d2[G_LOW]])
    while len(c0[STAGES]) > 1:
        gather.tick()

    g4 = tie(slot(r4, g_own[0]), [gather.last])
    gather.tick([g4], crossing=0)
    d3 = dict(backward_ffn(g4, s2, w), g_out=g4)
    sums = Sum(at)

    def pair(name):
        return [s3[name], s2[name]] if name in s3 else [d2[name], d3[name]]

    halves = [(c, c * PAGE) for c in range(per)]
    split = (pages // 2, pages - 1)

    def up_place(c):
        lane = 0 if c < split[0] else 1 if c < split[1] else 2
        return ((lane, 0, rows, (c - (0, split[0], split[1])[lane]) * rows),)

    heights, left = weight_grads(
        base, masks, "up_out_grad", [pair("ffn_in"), pair("g_pre"), pair("mixed"), pair("g_mid_low")],
        [(0, 1, c * PAGE, rows, up_place(c)) for c in range(pages)]
        + [(2, 3, column, rows, ((2, 0, rows, (pages - split[1] + c) * rows),)) for c, column in halves],
        joined=False,
    )
    t_left = sums.add(heights, *left)
    moved2 = sums.tick([t_left], [left, gather.last])
    moved3 = sums.tick([t_left], [moved2])
    most = 3 * fold // 4
    heights, right = weight_grads(
        base, masks, "down_grad", [pair("hidden"), tie(pair("g_out"), [left])],
        [(0, 1, column, fold, ((c, 0, most, 0), (2, most, fold - most, c * (fold - most)))) for c, column in halves],
    )
    t_right = sums.add(heights, *right)
    d3.update(backward_attention(d3, tie(x2, [right]), kb, vb, s2, w))
    moved4 = sums.tick([t_right], [right])
    gather.last = []
    while gather.flips:
        gather.tick([moved2])
    heights, rest = weight_grads(
        base, masks, "attention_grad",
        [pair(CONTEXT), pair("g_query"), [ma, s3[CONTEXT], mb, s2[CONTEXT]], pair("g_keys"), pair("g_values"),
         [table_rev, table_rev], pair("g_rel")],
        [(0, 1, column, rows, ((0, 0, rows, c * rows),)) for c, column in halves]
        + [(2, 3, column, rows, ((1, 0, rows, c * rows),)) for c, column in halves]
        + [(2, 4, column, rows, ((2, 0, rows, c * rows),)) for c, column in halves]
        + [(5, 6, column, rows, ((c, 0, rows, square),)) for c, column in halves],
        (2, [((0, 1), 0), ((0, 1), 1), ((2, 3), 1), ((2, 3), 0)]),
        [d2["sums"], d3["sums"], d2["ffn_sums"], d3["ffn_sums"]],
    )
    t_rest = sums.add(heights, *rest)
    own_out = jnp.stack([slot(y3, y2), slot(y2, y3)])
    low_grad = jnp.stack([d2[G_LOW], d3[G_LOW]])
    own_grad = jnp.stack([slot(d2["g_in"], d1["g_in"]), slot(d3["g_in"], d2["g_in"])])
    crossed = jnp.stack([slot(r3, r1), slot(r4, r2)])
    got_flip = at.move(tie(crossed, [moved4]), CORE)
    got_swap = at.move(tie(slot(low_grad, own_out), [rest, moved4]), SWAP)
    activations = jnp.where(at.home, own_out, slot(got_swap, got_flip))
    input_grads = jnp.where(at.home, own_grad, slot(got_flip, got_swap).astype(F32))
    moved5 = sums.tick([t_left, t_right], [moved3, moved4])
    sources, numbered = pieces_of([c0, c1, c2])
    taps = call(
        functools.partial(compression_kernel, masks, numbered, square, micro), "compression",
        places(AUTO, *tie(memory, [rest]), *sources),
        [((3 * (n // 2) * square, PAGE), BF, PIN)] * 2,
        [(whole, BF), ((width, PAGE), BF)], 0, base, 2 * SLACK,
    )
    t_comp = sums.add([square] * 3, *taps)
    moved6 = sums.tick([t_rest], [rest])
    moved7 = sums.tick([t_left, t_right, t_rest], [moved5, moved6])
    moved8 = sums.tick([t_comp], [taps, moved6])
    swap0 = sums.finish([t_left], [moved7, got_swap])
    moved9 = sums.tick([t_right, t_rest, t_comp], [moved7, moved8])
    moved10 = sums.tick([t_rest, t_comp], [moved9])
    sums.finish([t_right, t_rest, t_comp], [swap0, moved10])

    def unpage(item, start, count):
        block = item[OUT]
        parts = [block[(start + c) * rows : (start + c + 1) * rows] for c in range(count)]
        return jnp.concatenate(parts, 1)

    def lanes_of(group):
        return group[ITEMS]

    t_left, t_right, t_rest = lanes_of(t_left), lanes_of(t_right), lanes_of(t_rest)
    s_comp = jnp.stack([unpage(item, 0, per) for item in lanes_of(t_comp)])
    spans = (split[0], split[1] - split[0], pages - split[1])
    s_up = jnp.concatenate([unpage(item, 0, span) for item, span in zip(t_left, spans)], 1)
    s_out = unpage(t_left[2], spans[2], per)
    last = t_right[2][OUT]
    s_down = jnp.concatenate(
        [jnp.concatenate([t_right[c][OUT], last[c * (fold - most) : (c + 1) * (fold - most)]], 0) for c, _ in halves], 1
    )
    s_q, s_key, s_value = [unpage(item, 0, per) for item in t_rest]
    s_pos = jnp.concatenate([t_rest[c][OUT][square : square + rows] for c, _ in halves], 1)
    s_vec = t_rest[2][OUT][square:]
    s_norm = jnp.sum(
        q_weight[0].astype(F32) * s_q + key_weight[0].astype(F32) * s_key + value_weight[0].astype(F32) * s_value, 1
    ) / norm_gain[0].astype(F32)
    s_ffn = jnp.sum(up_weight[0].astype(F32) * s_up, 1) / ffn_gain[0].astype(F32)
    outs = (
        activations[:, None], input_grads[:, None], s_q, s_key, s_value, s_pos, s_out, s_up, s_down, s_comp, s_norm,
        s_vec[0, :rows], s_vec[1, :rows], s_ffn, s_vec[3, :fold], s_vec[2, :rows],
    )
    return tuple(o[None] for o in outs)


def solution(mesh):
    rows = P(SECTION, WIDE, None)
    vector = P(SECTION, WIDE)
    stream = P(SECTION, None, WIDE, None, None)
    taps = P(SECTION, None, WIDE, None)
    whole = P(None, WIDE, None, None)
    return jax.shard_map(
        shards,
        mesh=mesh,
        in_specs=(whole, stream, stream, whole) + (rows,) * 7 + (taps,) + (vector,) * 6,
        out_specs=(stream, stream) + (rows,) * 7 + (taps,) + (vector,) * 6,
        check_vma=False,
    )
```

```python
import functools

import jax
import jax.numpy as jnp
from jax import lax
from jax.experimental import pallas as pl
from jax.experimental.pallas import tpu as pltpu
from jax.sharding import PartitionSpec as P

HEADS = 8
HEAD_WIDTH = 128
MEM = 128
CMEM = 128
PAST = MEM + CMEM
SEG = 256
CNEW = 32
VISIBLE_KEYS = 512
PAGE = 512
VECTOR_ROWS = 16
STAGES = "stages"
PIECES = "pieces"
TERMS = "terms"
STEP = "step"
ITEMS = "items"
PARTS = "parts"
AUTO = "vmem"
PIN = "pin"
HBM = "hbm"
SECTION = "section"
WIDE = "wide"
G_LOW = "g_low"
SWAP = "swap"
CORE = "core"
OUT = "out"
CONTEXT = "context"
EPSILON = 1e-05
SCALE = HEAD_WIDTH ** (-0.5)
BF = jnp.bfloat16
F32 = jnp.float32
SLACK = 5 * 1024 * 1024


class Places:
    def __init__(self):
        self.n = lax.axis_size(WIDE)
        self.pair = self.n // 2
        self.bits = []
        bit = 1
        while bit < self.pair:
            self.bits.append(bit)
            bit *= 2
        self.wide = lax.axis_index(WIDE)
        self.core = lax.axis_index(SECTION)
        self.layer = self.wide // self.pair
        self.first = self.layer == 0
        self.home = self.core == self.layer
        self.base = self.wide ^ jnp.where(self.home, 0, self.pair)
        self.swap_pairs = [
            (s * self.n + w, (1 - s) * self.n + (w ^ self.pair))
            for s in range(2)
            for w in range(self.n)
            if s != w // self.pair
        ]

    def move(self, x, how):
        if how == SWAP:
            return lax.ppermute(x, (SECTION, WIDE), self.swap_pairs)
        if how == CORE:
            return lax.ppermute(x, SECTION, [(0, 1), (1, 0)])
        if how == "up":
            return lax.ppermute(x, WIDE, [(w, w + self.pair) for w in range(self.pair)])
        if how == "down":
            return lax.ppermute(x, WIDE, [(w + self.pair, w) for w in range(self.pair)])
        return lax.ppermute(x, WIDE, [(w, w ^ how) for w in range(self.n)])

    def lane_bits(self, lane):
        turn = lane * len(self.bits) // 3
        return self.bits[turn:] + self.bits[:turn]

    def summed_masks(self, lane):
        masks = [0]
        for bit in self.lane_bits(lane)[::-1] + [self.pair]:
            masks = masks + [m ^ bit for m in masks]
        return masks


def tie(values, after):
    after = [a for a in jax.tree.leaves(after)]
    return lax.optimization_barrier((values, after))[0] if after else values


def move_many(places, arrays, how):
    flat = [a.reshape(-1, a.shape[-1]) for a in arrays]
    moved = places.move(jnp.concatenate(flat, 0) if len(flat) > 1 else flat[0], how)
    parts, at = [], 0
    for a, f in zip(arrays, flat):
        parts.append(moved[at : at + f.shape[0]].reshape(a.shape))
        at += f.shape[0]
    return parts


class Gather:
    def __init__(self, places):
        self.places = places
        self.items = []
        self.flips = []
        self.last = []

    def add(self, lane, rows):
        item = dict(stages=self.places.lane_bits(lane), arr=rows[None], masks=[0], pieces=[], count=rows.shape[0])
        self.items.append(item)
        return item

    def tick(self, after=(), crossing=None, merge=True):
        at = self.places
        active = [item for item in self.items if item[STAGES]]
        tied = tie([item["arr"] for item in active], [self.last, after])
        last, groups, fresh = [], {}, []
        for item, arr in zip(active, tied):
            item["arr"] = arr
            groups.setdefault(item[STAGES][0], []).append(item)
        for how, members in groups.items():
            moved = move_many(at, [item["arr"] for item in members], how)
            last += moved
            for item, got in zip(members, moved):
                item[STAGES] = item[STAGES][1:]
                arr, masks = item["arr"], item["masks"]
                other = [m ^ how for m in masks]
                if item[STAGES]:
                    item["arr"], item["masks"] = jnp.concatenate([arr, got], 0), masks + other
                else:
                    self.flips.append((item, arr, masks))
                    fresh.append((item, got, other))
        count = len(self.flips) if crossing is None else crossing
        now, self.flips = self.flips[:count], self.flips[count:] + fresh
        flat = [arr.reshape(-1, PAGE) for _, arr, _ in now]
        if merge and now:
            got = at.move(tie(jnp.concatenate(flat, 0), [self.last, after]), CORE)
            last.append(got)
            ends = [sum(f.shape[0] for f in flat[:i]) for i in range(len(flat) + 1)]
            gots = [got[a:b] for a, b in zip(ends, ends[1:])]
        else:
            gots = []
            for f in flat:
                gots.append(at.move(tie(f, [self.last, after]), CORE))
            last += gots
        for (item, _, masks), arr, got in zip(now, flat, gots):
            item[PIECES] += [(arr, masks), (got, [m ^ at.pair for m in masks])]
        self.last = last
        return last

    def until(self, items, merge=True):
        while any(len(item[PIECES]) < 4 for item in items):
            self.tick(merge=merge)


class Sum:
    def __init__(self, places):
        self.places = places
        self.groups = []

    def add(self, heights, *parts):
        items = [dict(stages=self.places.lane_bits(lane), terms=[], out=None) for lane in range(len(heights))]
        group = dict(heights=heights, parts=parts, step=0, items=items)
        self.groups.append(group)
        return group

    def lanes(self, group, flat):
        quarter, parts, at = self.places.n // 4, [], 0
        for height in group["heights"]:
            parts.append(flat[at : at + quarter * height].reshape(quarter, height, PAGE))
            at += quarter * height
        return parts

    def total(self, terms, dtype):
        return sum(t.astype(F32) for t in terms).astype(dtype)

    def tick(self, groups, after=()):
        at = self.places
        going = [(group, item) for group in groups if group[STEP] > 0 for item in group[ITEMS] if item[STAGES]]
        crossing = [group for group in groups if group[STEP] == 0 or (group[STEP] == 1 and len(group[PARTS]) == 4)]
        operands = []
        for group, item in going:
            if group[STEP] == 1:
                operands.append(item["half"])
            else:
                half = item[TERMS][0].shape[0] // 2
                operands.append(self.total([t[half:] for t in item[TERMS]], BF))
                item[TERMS] = [t[:half] for t in item[TERMS]]
        sends = [group[PARTS][-1 - group[STEP]] for group in crossing]
        operands = tie(operands + sends, after)
        last, ways = [], {}
        for (group, item), operand in zip(going, operands):
            ways.setdefault(item[STAGES][0], []).append((item, operand))
        for how, members in ways.items():
            moved = move_many(at, [operand for _, operand in members], how)
            last += moved
            for (item, _), got in zip(members, moved):
                item[STAGES] = item[STAGES][1:]
                item[TERMS].append(got)
        for group, operand in zip(crossing, operands[len(going) :]):
            got = at.move(operand, CORE)
            last.append(got)
            if len(group[PARTS]) == 2:
                rows = got.shape[0] // 2
                pairs = [(group[PARTS][0][:rows], got[:rows]), (group[PARTS][0][rows:], got[rows:])]
            else:
                pairs = [None, None]
                pairs[1 - group[STEP]] = (group[PARTS][1 - group[STEP]], got)
            if pairs[0]:
                for item, a, b in zip(group[ITEMS], *[self.lanes(group, p) for p in pairs[0]]):
                    item[TERMS] += [a, b]
            if pairs[1]:
                for item, a, b in zip(group[ITEMS], *[self.lanes(group, p) for p in pairs[1]]):
                    item["half"] = self.total([a, b], BF)
        for group in groups:
            group[STEP] += 1
        return last

    def finish(self, groups, after=()):
        at = self.places
        items = [item for group in groups for item in group[ITEMS]]
        while any(item[STAGES] for item in items):
            self.tick([group for group in groups if any(item[STAGES] for item in group[ITEMS])])
        finals = [self.total(item[TERMS], F32)[0] for item in items]
        moved = move_many(at, tie([a.astype(BF) for a in finals], after), SWAP)
        for item, a, got in zip(items, finals, moved):
            item[OUT] = jnp.where(at.home, a, got.astype(F32))
        return moved


def mm(a, b):
    return jnp.dot(a, b, preferred_element_type=F32)


def mm_nt(a, b):
    return lax.dot_general(a, b, (((1,), (1,)), ((), ())), preferred_element_type=F32)


def mm_tn(a, b):
    return lax.dot_general(a, b, (((0,), (0,)), ((), ())), preferred_element_type=F32)


def statistics(rows):
    average = jnp.mean(rows, -1, keepdims=True)
    centered = rows - average
    inverse = lax.rsqrt(jnp.mean(centered * centered, -1, keepdims=True) + EPSILON)
    return centered * inverse, inverse


def norm_back(grad_hat, normed, inverse):
    first = jnp.mean(grad_hat, -1, keepdims=True)
    second = jnp.mean(grad_hat * normed, -1, keepdims=True)
    return inverse * (grad_hat - first - normed * second)


def relative_table(inv_freq, reverse):
    step = jnp.arange(VISIBLE_KEYS) if reverse else VISIBLE_KEYS - 1 - jnp.arange(VISIBLE_KEYS)
    angles = step.astype(F32)[:, None] * inv_freq[None, :]
    return jnp.concatenate([jnp.sin(angles), jnp.cos(angles)], axis=1).astype(BF)


def columns(at):
    return slice(at * PAGE, (at + 1) * PAGE)


class Copies:
    def __init__(self, sems):
        self.sems = sems
        self.used = 0
        self.open = []

    def start(self, source, target):
        copy = pltpu.make_async_copy(source, target, self.sems.at[self.used])
        copy.start()
        self.used += 1
        self.open.append(copy)
        return copy

    def wait(self, copies=None):
        for copy in self.open[:] if copies is None else copies:
            copy.wait()
            self.open.remove(copy)


def pack_kernel(first_ref, *refs):
    (q, key, value, pos, out, up, down, comp, cmems, memories, inputs, cotangent, vectors) = refs[:13]
    pack_a, pack_b, pack_s, pack_t = refs[13:17]
    copies = Copies(refs[17])
    rows, fold = q.shape[0], down.shape[0]

    def put(target, at, source, count):
        for c in range(source.shape[-1] // PAGE):
            copies.start(source.at[:, columns(c)], target.at[pl.ds(at, count)])
            at += count
        return at

    def either(target, row):
        sem = copies.sems.at[copies.used]
        copies.used += 1

        @pl.when(first_ref[0] == 1)
        def _():
            pltpu.make_async_copy(cotangent.at[row], target, sem).start()

        @pl.when(first_ref[0] == 0)
        def _():
            pltpu.make_async_copy(inputs.at[row], target, sem).start()

        copies.open.append(pltpu.make_async_copy(inputs.at[row], target, sem))

    at = put(pack_a, 0, q, rows) + VECTOR_ROWS
    for source in (key, value):
        at = put(pack_a, at, source, rows)
    put(pack_a, at, pos, rows)
    at = put(pack_b, 0, up, rows)
    at = put(pack_b, at, down, fold)
    put(pack_b, at, out, rows)
    at = 0
    for i in range(memories.shape[0]):
        for source in (cmems, memories):
            copies.start(source.at[i], pack_s.at[pl.ds(at, source.shape[1])])
            at += source.shape[1]
    either(pack_s.at[pl.ds(at, SEG)], 0)
    at = 0
    for i in range(1, inputs.shape[0]):
        either(pack_t.at[pl.ds(at, SEG)], i)
        at += SEG
    for t in range(3):
        copies.start(comp.at[t], pack_t.at[pl.ds(at, rows)])
        at += rows
    start = q.shape[1] // PAGE * rows
    pack_a[start : start + VECTOR_ROWS, :] = vectors[...].astype(BF)
    copies.wait()


def put_blocks(base, source, count, masks, first, rows, target, column):
    for i, mask in enumerate(masks):
        at = pl.multiple_of((base ^ mask) * rows, rows)
        target[pl.ds(at, rows), column : column + PAGE] = source[i * count + first : i * count + first + rows, :]


def assemble_kernel(items, base_ref, *refs):
    base = base_ref[0]
    sources = sum(len(masks) for masks, _, _ in items)
    at = 0
    for masks, count, parts in items:
        for first, rows, out, column in parts:
            for i, blocks in enumerate(masks):
                put_blocks(base, refs[at + i], count, blocks, first, rows, refs[sources + out], column)
        at += len(masks)


def prepare_kernel(memory, vecs, table, table_rev, key, value, pos0, pos1, context0, context1, kmem0, vmem0, kmem1, vmem1, rel,
                   rel_rev, ctx, sems):
    copies = Copies(sems)
    ctx[...] = (statistics(memory[...].astype(F32))[0] * vecs[0:1, :]).astype(BF)
    for h, context in enumerate((context0, context1)):
        copies.start(ctx.at[pl.ds(h * PAST, PAST)], context)
    for h in range(2):
        rows = slice(h * PAST, (h + 1) * PAST)
        (kmem0, kmem1)[h][...] = mm(ctx[rows, :], key[...]).astype(BF)
        (vmem0, vmem1)[h][...] = mm(ctx[rows, :], value[...]).astype(BF)
    for c, pos in enumerate((pos0, pos1)):
        rel[:, columns(c)] = mm(table[...], pos[...]).astype(BF)
        rel_rev[:, columns(c)] = mm(table_rev[...], pos[...]).astype(BF)
    copies.wait()


def forward_attention_kernel(x, kmem, vmem, rel, vecs, q, key, value, context, q_content, q_position, kx, vx, probs,
                             mixed, ctx, sems):
    copies = Copies(sems)
    ctx[...] = (statistics(x[...].astype(F32))[0] * vecs[0:1, :]).astype(BF)
    copies.start(ctx, context)
    for h in range(2):
        query = mm(ctx[...], q[:, columns(h)])
        q_content[:, columns(h)] = ((query + vecs[1:2, columns(h)]) * SCALE).astype(BF)
        q_position[:, columns(h)] = ((query + vecs[2:3, columns(h)]) * SCALE).astype(BF)
        kx[:, columns(h)] = mm(ctx[...], key[:, columns(h)]).astype(BF)
        vx[:, columns(h)] = mm(ctx[...], value[:, columns(h)]).astype(BF)
    row = lax.broadcasted_iota(jnp.int32, (SEG, VISIBLE_KEYS), 0)
    col = lax.broadcasted_iota(jnp.int32, (SEG, VISIBLE_KEYS), 1)
    allowed = col <= row + PAST
    for h in range(HEADS):
        hs = slice(h * HEAD_WIDTH, (h + 1) * HEAD_WIDTH)
        qc, qp = q_content[:, hs], q_position[:, hs]
        scores = jnp.concatenate([mm_nt(qc, kmem[:, hs]), mm_nt(qc, kx[:, hs])], 1)
        position = pltpu.roll(mm_nt(qp, rel[:, hs]), VISIBLE_KEYS - SEG + 1, 1, stride=1, stride_axis=0)
        scores = jnp.where(allowed, scores + position, -1e30)
        weight = jnp.exp(scores - jnp.max(scores, -1, keepdims=True))
        low = (weight * (1.0 / jnp.sum(weight, -1, keepdims=True))).astype(BF)
        probs[h] = low
        mixed[:, hs] = (mm(low[:, :PAST], vmem[:, hs]) + mm(low[:, PAST:], vx[:, hs])).astype(BF)
    copies.wait()


def forward_ffn_kernel(keep, x, mixed, vecs, up_bias, out, up0, up1, down0, down1, y, *refs):
    if keep:
        normed2, inverse2, ffn_in, hidden, slope, middle, inner, acts, sems = refs
        copies = Copies(sems)
    else:
        middle, inner, acts = refs
    for h in range(2):
        middle[:, columns(h)] = x[:, columns(h)].astype(F32) + mm(mixed[...], out[:, columns(h)])
    normed, inverse = statistics(middle[...])
    inner[...] = (normed * vecs[3:4, :]).astype(BF)
    if keep:
        normed2[...] = normed
        inverse2[...] = jnp.broadcast_to(inverse, inverse2.shape)
        copies.start(inner, ffn_in)
    left = up0.shape[1] // PAGE

    def expand(source, here, there):
        pre = mm(inner[...], source[:, here]) + up_bias[0:1, there]
        cdf = 0.5 * (1.0 + lax.erf(pre * 0.7071067811865476))
        acts[:, there] = (pre * cdf).astype(BF)
        if keep:
            slope[:, there] = (cdf + pre * (jnp.exp(-0.5 * pre * pre) * 0.3989422804014327)).astype(BF)

    if keep:
        for c in range(acts.shape[1] // PAGE):
            expand(*((up0, columns(c)) if c < left else (up1, columns(c - left))), columns(c))
    else:
        for source, first in ((up0, 0), (up1, left)):

            def body(c, carry, source=source, first=first):
                here = pl.ds(pl.multiple_of(c * PAGE, PAGE), PAGE)
                expand(source, here, pl.ds(pl.multiple_of((first + c) * PAGE, PAGE), PAGE))
                return carry

            lax.fori_loop(0, source.shape[1] // PAGE, body, 0)
    if keep:
        copies.start(acts, hidden)
    for h, down in enumerate((down0, down1)):
        y[:, columns(h)] = (middle[:, columns(h)] + mm(acts[...], down[...]) + vecs[4:5, columns(h)]).astype(BF)
    if keep:
        copies.wait()


def backward_ffn_kernel(g, slope, normed2, inverse2, vecs, out, up0, up1, down0, down1, g_pre, g_mid, g_mid_low,
                        g_mixed, sums, pre, low, sems):
    copies = Copies(sems)
    sums[...] = jnp.zeros_like(sums)
    for c in range(slope.shape[1] // PAGE):
        g_hidden = mm_nt(g[:, columns(0)], down0[columns(c), :]) + mm_nt(g[:, columns(1)], down1[columns(c), :])
        g_low = (g_hidden * slope[:, columns(c)].astype(F32)).astype(BF)
        pre[:, columns(c)] = g_low
        sums[0:1, columns(c)] = jnp.sum(g_low.astype(F32), 0, keepdims=True)
    copies.start(pre, g_pre)
    g_out = g[...].astype(F32)
    sums[1:2, : g.shape[1]] = jnp.sum(g_out, 0, keepdims=True)
    half = up0.shape[1]
    g_ffn = mm_nt(pre[:, :half], up0[...]) + mm_nt(pre[:, half:], up1[...])
    g_middle = g_out + norm_back(g_ffn * vecs[3:4, :], normed2[...], inverse2[:, 0:1])
    g_mid[...] = g_middle
    low[...] = g_middle.astype(BF)
    copies.start(low, g_mid_low)
    g_mixed[...] = mm_nt(low[...], out[...]).astype(BF)
    copies.wait()


def backward_attention_kernel(g_mixed, g_mid, x, q_content, q_position, kmem, kx, vmem, vx, probs, rel_rev, vecs, q,
                              key, value, g_in, g_low, g_query, g_keys, g_values, g_rel, sums, total, query, keys,
                              values, rels, sems):
    copies = Copies(sems)
    row = lax.broadcasted_iota(jnp.int32, (VISIBLE_KEYS, VISIBLE_KEYS), 0)
    col = lax.broadcasted_iota(jnp.int32, (VISIBLE_KEYS, VISIBLE_KEYS), 1)
    flip = jnp.where(row + col == VISIBLE_KEYS - 1, 1.0, 0.0).astype(BF)
    sums[...] = jnp.zeros_like(sums)
    for h in range(HEADS):
        hs = slice(h * HEAD_WIDTH, (h + 1) * HEAD_WIDTH)
        gm, low = g_mixed[:, hs], probs[h]
        g_probs = jnp.concatenate([mm_nt(gm, vmem[:, hs]), mm_nt(gm, vx[:, hs])], 1)
        values[:, hs] = mm_tn(low, gm).astype(BF)
        p = low.astype(F32)
        g_scores = (p * (g_probs - jnp.sum(g_probs * p, -1, keepdims=True))).astype(BF)
        keys[:, hs] = mm_tn(g_scores, q_content[:, hs]).astype(BF)
        g_qc = mm(g_scores[:, :PAST], kmem[:, hs]) + mm(g_scores[:, PAST:], kx[:, hs])
        turned = pltpu.roll(mm(g_scores, flip), VISIBLE_KEYS - SEG + 1, 1, stride=1, stride_axis=0).astype(BF)
        g_qp = mm(turned, rel_rev[:, hs])
        rels[:, hs] = mm_tn(turned, q_position[:, hs]).astype(BF)
        sums[0:1, hs] = jnp.sum(g_qc, 0, keepdims=True) * SCALE
        sums[1:2, hs] = jnp.sum(g_qp, 0, keepdims=True) * SCALE
        query[:, hs] = ((g_qc + g_qp) * SCALE).astype(BF)
    for source, target in ((query, g_query), (keys, g_keys), (values, g_values), (rels, g_rel)):
        copies.start(source, target)
    g_context = mm_nt(query[...], q[...]) + mm_nt(keys[PAST:, :], key[...]) + mm_nt(values[PAST:, :], value[...])
    normed, inverse = statistics(x[...].astype(F32))
    g_x = g_mid[...] + norm_back(g_context * vecs[0:1, :], normed, inverse)
    total[...] = g_x
    copies.start(total, g_in)
    g_low[...] = g_x.astype(BF)
    copies.wait()


def views_of(outs):
    if len(outs) == 4:
        return [(out, 0) for out in outs]
    return [(out, half * (out.shape[0] // 2)) for out in outs for half in range(2)]


def scatter_blocks(base, masks, source, outs, start, height, first, rows, cut, at):
    quarter = len(masks) // 4
    for j, mask in enumerate(masks):
        where = pl.multiple_of((base ^ mask) * rows + first, 16)
        out, origin = views_of(outs)[j // quarter]
        row = origin + start + (j % quarter) * height + at
        out[row : row + cut, :] = source[pl.ds(where, cut), :]


def weight_kernel(loads, parts, vector_place, masks, heights, count, shapes, made, base_ref, *refs):
    base = base_ref[0]
    n, quarter = len(masks[0]), len(masks[0]) // 4
    ins, outs = refs[:count], refs[count : count + made]
    stacks = refs[count + made : count + made + len(shapes)]
    scratch = refs[count + made + len(shapes)]
    copies = Copies(refs[-1])
    starts = [quarter * sum(heights[:lane]) for lane in range(len(masks))]
    waiting = {}
    for number, stack, first in loads:
        target = stacks[stack].at[pl.ds(first, ins[number].shape[0])]
        waiting.setdefault(stack, []).append(copies.start(ins[number], target))
    if vector_place is not None:
        lane, at, sources = vector_place
        vector = refs[-2]
        vector[...] = jnp.zeros_like(vector)
        for i, (numbers, row) in enumerate(sources):
            total = ins[numbers[0]][row : row + 1, :] + ins[numbers[1]][row : row + 1, :]
            size = (total.shape[1] if i == 3 else shapes[0][1]) // n
            for w in range(n):
                vector[w, i : i + 1, :size] = total[:, w * size : (w + 1) * size]
        for j, mask in enumerate(masks[lane]):
            out, origin = views_of(outs)[j // quarter]
            to = origin + starts[lane] + (j % quarter) * heights[lane] + at
            out[to : to + VECTOR_ROWS, :] = vector[base ^ mask].astype(BF)
    for left, right, column, rows, spots in parts:
        for stack in (left, right):
            copies.wait(waiting.pop(stack, []))
        chunk = 1024
        for start in range(0, n * rows, chunk):
            product = mm_tn(stacks[left][:, start : start + chunk], stacks[right][:, column : column + PAGE])
            scratch[start : start + chunk, :] = product.astype(BF)
        for lane, first, cut, at in spots:
            scatter_blocks(base, masks[lane], scratch, outs, starts[lane], heights[lane], first, rows, cut, at)


def compression_kernel(masks, pieces, count, streams, base_ref, *refs):
    base = base_ref[0]
    sources = sum(len(blocks) for blocks in pieces)
    rows_of, ins, outs = refs[:streams], refs[streams : streams + sources], refs[streams + sources : streams + sources + 2]
    weight, scratch = refs[streams + sources + 2 :]
    width = weight.shape[0]
    n = len(masks[0])
    rows = width // n
    old = [[], [], []]
    row = lax.broadcasted_iota(jnp.int32, (CNEW, MEM), 0)
    col = lax.broadcasted_iota(jnp.int32, (CNEW, MEM), 1)
    for ref in rows_of:
        for t in range(3):
            pick = jnp.where(col == 3 * row + t, 1.0, 0.0).astype(BF)
            old[t].append(mm(pick, ref[CMEM:, :]).astype(BF))
    old = [jnp.concatenate(o, 0) for o in old]

    def load(t):
        at = sum(len(blocks) for blocks in pieces[:t])
        for i, blocks in enumerate(pieces[t]):
            for h in range(width // PAGE):
                put_blocks(base, ins[at + i], count, blocks, h * rows, rows, weight, h * PAGE)

    squeezed = jnp.zeros(old[0].shape, F32)
    for t in range(3):
        load(t)
        squeezed = squeezed + mm(old[t], weight[...])
    squeezed = squeezed.astype(BF)
    g_rebuilt, g_squeezed = [], jnp.zeros(old[0].shape, F32)
    for t in range(3):
        load(t)
        rebuilt = mm_nt(squeezed, weight[...])
        g_rebuilt.append(((rebuilt - old[t].astype(F32)) * (2.0 / (3 * CNEW))).astype(BF))
        g_squeezed = g_squeezed + mm(g_rebuilt[t], weight[...])
    right = jnp.concatenate([squeezed, g_squeezed.astype(BF)], 0)
    height = width // PAGE * rows
    for t in range(3):
        left = jnp.concatenate([g_rebuilt[t], old[t]], 0)
        for h in range(width // PAGE):
            scratch[...] = mm_tn(left, right[:, columns(h)]).astype(BF)
            scatter_blocks(base, masks[t], scratch, outs, t * (n // 4) * height, height, 0, rows, rows, h * rows)


def size_of(shape, dtype):
    total = jnp.dtype(dtype).itemsize
    for s in shape:
        total *= s
    return total


def call(kernel, name, arrays, outs, scratch=(), copies=0, base=None, slack=SLACK, cost=2 * 10**9):
    held = sum(size_of(a.shape, a.dtype) for a, place in arrays if place == AUTO)
    held += sum(size_of(s, d) for s, d, place in outs if place == AUTO) + sum(size_of(*s) for s in scratch)
    specs = dict(vmem=pltpu.VMEM, pin=pltpu.VMEM, hbm=pltpu.HBM)
    shapes = dict(vmem=jax.ShapeDtypeStruct, pin=pltpu.VMEM, hbm=pltpu.HBM)

    def placed(a, place):
        return a if place == AUTO else pltpu.with_memory_space_constraint(a, specs[place])

    scalars = [] if base is None else [base]
    return pl.pallas_call(
        kernel,
        out_shape=[shapes[place](s, d) for s, d, place in outs],
        in_specs=[pl.BlockSpec(memory_space=pltpu.SMEM)] * len(scalars)
        + [pl.BlockSpec(memory_space=specs[place]) for _, place in arrays],
        out_specs=[pl.BlockSpec(memory_space=specs[place]) for _, _, place in outs],
        scratch_shapes=[pltpu.VMEM(*s) for s in scratch] + ([pltpu.SemaphoreType.DMA((copies,))] if copies else []),
        compiler_params=pltpu.CompilerParams(vmem_limit_bytes=held + slack),
        cost_estimate=pl.CostEstimate(flops=cost, bytes_accessed=1, transcendentals=0),
        name=name,
    )(*scalars, *[placed(a, place) for a, place in arrays])


def places(kind, *arrays):
    return [(a, kind) for a in arrays]


def forward_attention(x, kmem, vmem, w):
    seg = (SEG, x.shape[1])
    got = call(
        forward_attention_kernel, "forward_attention",
        places(AUTO, x) + places(PIN, kmem, vmem, w["rel"], w["vecs"], w["q"], w["key"], w["value"]),
        [(seg, BF, HBM)] + [(seg, BF, PIN)] * 4 + [((HEADS, SEG, VISIBLE_KEYS), BF, PIN), (seg, BF, PIN)],
        [(seg, BF)], 1,
    )
    return dict(zip((CONTEXT, "q_content", "q_position", "kx", "vx", "probs", "mixed"), got))


def forward_ffn(x, s, w, keep=True):
    seg, wide = (SEG, x.shape[1]), (SEG, w["up_bias"].shape[1])
    outs = [(seg, BF, AUTO)]
    if keep:
        outs += [(seg, F32, PIN), ((SEG, 128), F32, PIN), (seg, BF, HBM), (wide, BF, HBM), (wide, BF, PIN)]
    got = call(
        functools.partial(forward_ffn_kernel, keep), "forward_ffn",
        places(AUTO, x)
        + places(PIN, s["mixed"], w["vecs"], w["up_bias"], w[OUT], w["up0"], w["up1"], w["down0"], w["down1"]),
        outs, [(seg, F32), (seg, BF), (wide, BF)], 2 if keep else 0,
    )
    return got[0], dict(s, **dict(zip(("normed2", "inverse2", "ffn_in", "hidden", "slope"), got[1:])))


def backward_ffn(g, s, w):
    seg, wide = g.shape, s["slope"].shape
    got = call(
        backward_ffn_kernel, "backward_ffn",
        places(AUTO, g)
        + places(PIN, s["slope"], s["normed2"], s["inverse2"], w["vecs"], w[OUT], w["up0"], w["up1"], w["down0"],
                 w["down1"]),
        [(wide, BF, HBM), (seg, F32, PIN), (seg, BF, HBM), (seg, BF, PIN), ((8, wide[1]), F32, AUTO)],
        [(wide, BF), (seg, BF)], 2,
    )
    return dict(zip(("g_pre", "g_mid", "g_mid_low", "g_mixed", "ffn_sums"), got))


def backward_attention(d, x, kmem, vmem, s, w, cost=2 * 10**9):
    seg, keys = x.shape, (VISIBLE_KEYS, x.shape[1])
    got = call(
        backward_attention_kernel, "backward_attention",
        places(PIN, d["g_mixed"], d["g_mid"]) + places(AUTO, x)
        + places(PIN, s["q_content"], s["q_position"], kmem, s["kx"], vmem, s["vx"], s["probs"], w["rel_rev"],
                 w["vecs"], w["q"], w["key"], w["value"]),
        [(seg, F32, HBM), (seg, BF, AUTO), (seg, BF, HBM), (keys, BF, HBM), (keys, BF, HBM), (keys, BF, HBM),
         ((8, seg[1]), F32, AUTO)],
        [(seg, F32), (seg, BF), (keys, BF), (keys, BF), (keys, BF)], 5, cost=cost,
    )
    return dict(zip(("g_in", G_LOW, "g_query", "g_keys", "g_values", "g_rel", "sums"), got))


def weight_grads(base, masks, name, stacks, parts, vectors=None, extra=(), joined=False):
    n = len(masks[0])
    heights = [0] * len(masks)
    for part in parts:
        for lane, _, rows, at in part[-1]:
            heights[lane] = max(heights[lane], at + rows)
    place = None
    if vectors is not None:
        place = (vectors[0], heights[vectors[0]], vectors[1])
        heights[vectors[0]] += VECTOR_ROWS
    arrays, loads, shapes = places(AUTO, *extra), [], []
    for i, stack in enumerate(stacks):
        at = 0
        for a in stack:
            loads.append((len(arrays), i, at))
            arrays.append((a, HBM))
            at += a.shape[0]
        shapes.append((at, stack[0].shape[1]))
    tallest = max([n * p[3] for p in parts])
    scratch = [(s, BF) for s in shapes] + [((tallest, PAGE), BF)]
    if vectors is not None:
        scratch.append(((n, VECTOR_ROWS, PAGE), F32))
    got = call(
        functools.partial(weight_kernel, loads, parts, place, masks, heights, len(arrays), shapes, 2 if joined else 4),
        name, arrays, [((n // (2 if joined else 4) * sum(heights), PAGE), BF, PIN)] * (2 if joined else 4), scratch, len(loads), base, 2 * SLACK, 1,
    )
    return heights, got


def pieces_of(items):
    return [piece for item in items for piece, _ in item[PIECES]], [[m for _, m in item[PIECES]] for item in items]


def assemble(base, name, items, parts, shapes):
    arrays, masks = pieces_of(items)
    plan = [(m, item["count"], p) for m, item, p in zip(masks, items, parts)]
    return call(
        functools.partial(assemble_kernel, plan), name, places(AUTO, *arrays), [(s, BF, PIN) for s in shapes],
        base=base,
    )


def shards(
    inputs, memories, cmems, cotangent, q_weight, key_weight, value_weight, pos_weight, out_weight, up_weight,
    down_weight, comp_weight, norm_gain, content_bias, position_bias, ffn_gain, up_bias, down_bias,
):
    at = Places()
    first = at.first
    width = q_weight.shape[-1]
    ff = up_weight.shape[-1]
    rows = q_weight.shape[1]
    n = at.n
    fold = ff // n
    per, pages = width // PAGE, ff // PAGE
    base = at.base.reshape(1).astype(jnp.int32)
    masks = [at.summed_masks(lane) for lane in range(3)]
    square = per * rows
    seam = 3 * pages // 4

    micro = memories.shape[1]
    kept = micro * PAST
    sizes = [
        (4 * square + VECTOR_ROWS, PAGE), (pages * rows + per * fold + square, PAGE), (kept + SEG, width),
        ((micro - 1) * SEG + 3 * rows, width),
    ]
    vectors = [
        jnp.pad(v.astype(F32), ((0, 0), (0, PAGE - v.shape[1])))
        for v in (norm_gain, content_bias, position_bias, ffn_gain, down_bias, up_bias)
    ]
    vectors = jnp.pad(jnp.concatenate(vectors, 0), ((0, VECTOR_ROWS - len(vectors)), (0, 0)))
    pack_a, pack_b, pack_s, pack_t = call(
        pack_kernel, "pack",
        places(HBM, q_weight[0], key_weight[0], value_weight[0], pos_weight[0], out_weight[0], up_weight[0],
               down_weight[0], comp_weight[0], cmems[0, :, 0], memories[0, :, 0], inputs[:, 0], cotangent[:, 0])
        + places(AUTO, vectors),
        [(size, BF, AUTO) for size in sizes], (), 5 * per + pages + per + 3 * micro + 3,
        jnp.where(first, 1, 0).reshape(1).astype(jnp.int32),
    )

    def swapped(x, after):
        x = tie(x, after)
        got = at.move(x, SWAP)
        return jnp.where(at.home, x, got), got

    def slot(a, b):
        return jnp.where(first, a, b)

    gather = Gather(at)
    pack_a, got_a = swapped(pack_a, [])
    cuts = [square + VECTOR_ROWS, 2 * square + VECTOR_ROWS, 3 * square + VECTOR_ROWS]
    pos_rows = pack_a[cuts[2] :]
    a0 = gather.add(0, pack_a[: cuts[0]])
    a1 = gather.add(1, jnp.concatenate([pack_a[cuts[0] : cuts[1]], pos_rows[:rows]], 0))
    a2 = gather.add(2, jnp.concatenate([pack_a[cuts[1] : cuts[2]], pos_rows[rows:]], 0))
    pack_b, got_b = swapped(pack_b, [got_a])
    while len(a0[STAGES]) > 1:
        gather.tick()
    moved = gather.tick()
    pack_s = tie(pack_s, [got_b, moved])
    got_s = at.move(pack_s, SWAP)
    memory = [jnp.where(at.home, pack_s[s], got_s[s]) for s in [slice(i * PAST, (i + 1) * PAST) for i in range(micro)]]
    x_own = [jnp.where(at.home, inputs[0, 0], got_s[kept:])]
    g_own = [jnp.where(at.home, cotangent[0, 0], got_s[kept:])]
    b2 = gather.add(2, pack_b[: seam * rows])
    b1 = gather.add(1, pack_b[seam * rows : pages * rows + fold])
    b0 = gather.add(0, pack_b[pages * rows + fold :])
    gather.tick()
    while len(b0[STAGES]) > 1:
        moved = gather.tick()
    pack_t = tie(pack_t, [got_s])
    got_t = at.move(pack_t, SWAP)
    x_own.append(jnp.where(at.home, inputs[1, 0], got_t[:SEG]))
    g_own.append(jnp.where(at.home, cotangent[1, 0], got_t[:SEG]))
    comp = jnp.where(at.home, pack_t[SEG:], got_t[SEG:])

    gather.until([a0, a1, a2])
    whole = (width, width)
    w = {}
    spread = [(c * rows, rows, 0, c * PAGE) for c in range(per)]

    def spread_to(out):
        return [(c * rows, rows, out, c * PAGE) for c in range(per)]

    w["q"], w["key"], w["value"], pos0, pos1 = assemble(
        base, "assemble_attention", [a0, a1, a2],
        [spread_to(0), spread_to(1) + [(square, rows, 3, 0)], spread_to(2) + [(square, rows, 4, 0)]],
        [whole] * 3 + [(width, PAGE)] * 2,
    )
    all_masks = [m for _, ms in a0[PIECES] for m in ms]
    order = jnp.array([all_masks.index(m) for m in range(n)], jnp.int32)[jnp.arange(n) ^ at.base]
    flat = [piece.reshape(len(ms), a0["count"], PAGE)[:, square:] for piece, ms in a0[PIECES]]
    flat = jnp.take(jnp.concatenate(flat, 0), order, axis=0).astype(F32)
    w["vecs"] = flat[:, :8, :rows].transpose(1, 0, 2).reshape(8, width)
    w["up_bias"] = flat[:, 5, :fold].reshape(1, ff)
    inv_freq = tie(1.0 / 10000.0 ** (jnp.arange(0, width, 2).astype(F32) / width), [moved])
    table, table_rev = relative_table(inv_freq, False), relative_table(inv_freq, True)
    past, keys, mem = (micro * PAST, width), (VISIBLE_KEYS, width), (PAST, width)
    slots = jnp.concatenate([slot(memory[0], memory[1]), slot(memory[1], memory[0])], 0)
    ma, mb, ka, va, kb, vb, w["rel"], w["rel_rev"] = call(
        prepare_kernel, "prepare",
        places(AUTO, slots, w["vecs"], table, table_rev) + places(PIN, w["key"], w["value"], pos0, pos1),
        [(mem, BF, HBM)] * 2 + [(mem, BF, PIN)] * 4 + [(keys, BF, PIN)] * 2, [(past, BF)], 2,
    )
    s1 = forward_attention(x_own[0], ka, va, w)
    gather.tick(crossing=1, merge=False)
    gather.tick([s1["mixed"]], merge=False)
    gather.until([b0, b1, b2])
    w["up0"], w["up1"], w["down0"], w["down1"], w[OUT] = assemble(
        base, "assemble_ffn", [b2, b1, b0],
        [
            [(c * rows, rows, 0, c * PAGE) for c in range(seam)],
            [(c * rows, rows, 1, c * PAGE) for c in range(pages - seam)] + [((pages - seam) * rows, fold, 2, 0)],
            [(0, fold, 3, 0)] + [(fold + c * rows, rows, 4, c * PAGE) for c in range(per)],
        ],
        [(width, seam * PAGE), (width, (pages - seam) * PAGE), (ff, PAGE), (ff, PAGE), whole],
    )

    y1, _ = forward_ffn(x_own[0], s1, w, False)
    r1 = at.move(y1, "up")
    x2 = slot(x_own[1], r1)
    y2, s2 = forward_ffn(x2, forward_attention(x2, kb, vb, w), w)
    r2 = at.move(y2, "up")

    d1 = dict(backward_ffn(g_own[0], s2, w), g_out=g_own[0])
    d1.update(backward_attention(d1, x2, kb, vb, s2, w))
    r3 = at.move(d1[G_LOW], "down")
    x3 = tie(slot(x_own[0], r2), [d1[G_LOW]])
    y3, s3 = forward_ffn(x3, forward_attention(x3, ka, va, w), w)
    g3 = tie(slot(r3, g_own[1]), [y3])
    d2 = dict(backward_ffn(g3, s3, w), g_out=g3)
    d2.update(backward_attention(d2, x3, ka, va, s3, w))
    r4 = at.move(d2[G_LOW], "down")

    c0, c1, c2 = [
        gather.add(t, jnp.concatenate([comp[t * rows : (t + 1) * rows, columns(c)] for c in range(per)], 0))
        for t in range(3)
    ]
    gather.last = []
    gather.tick([d2[G_LOW]])
    while len(c0[STAGES]) > 1:
        gather.tick()

    g4 = tie(slot(r4, g_own[0]), [gather.last])
    gather.tick([g4], crossing=0)
    d3 = dict(backward_ffn(g4, s2, w), g_out=g4)
    sums = Sum(at)

    def pair(name):
        return [s3[name], s2[name]] if name in s3 else [d2[name], d3[name]]

    halves = [(c, c * PAGE) for c in range(per)]
    split = (pages // 2, pages - 1)

    def up_place(c):
        lane = 0 if c < split[0] else 1 if c < split[1] else 2
        return ((lane, 0, rows, (c - (0, split[0], split[1])[lane]) * rows),)

    heights, left = weight_grads(
        base, masks, "up_out_grad", [pair("ffn_in"), pair("g_pre"), pair("mixed"), pair("g_mid_low")],
        [(0, 1, c * PAGE, rows, up_place(c)) for c in range(pages)]
        + [(2, 3, column, rows, ((2, 0, rows, (pages - split[1] + c) * rows),)) for c, column in halves],
        joined=False,
    )
    t_left = sums.add(heights, *left)
    moved2 = sums.tick([t_left], [left, gather.last])
    moved3 = sums.tick([t_left], [moved2])
    most = 3 * fold // 4
    heights, right = weight_grads(
        base, masks, "down_grad", [pair("hidden"), tie(pair("g_out"), [left])],
        [(0, 1, column, fold, ((c, 0, most, 0), (2, most, fold - most, c * (fold - most)))) for c, column in halves],
    )
    t_right = sums.add(heights, *right)
    d3.update(backward_attention(d3, tie(x2, [right]), kb, vb, s2, w, 1))
    moved4 = sums.tick([t_right], [right])
    gather.last = []
    while gather.flips:
        gather.tick([moved2])
    heights, rest = weight_grads(
        base, masks, "attention_grad",
        [pair(CONTEXT), [d2["g_query"], tie(d3["g_query"], moved3)], [ma, s3[CONTEXT], mb, s2[CONTEXT]], pair("g_keys"), pair("g_values"),
         [table_rev, table_rev], pair("g_rel")],
        [(0, 1, column, rows, ((0, 0, rows, c * rows),)) for c, column in halves]
        + [(2, 3, column, rows, ((1, 0, rows, c * rows),)) for c, column in halves]
        + [(2, 4, column, rows, ((2, 0, rows, c * rows),)) for c, column in halves]
        + [(5, 6, column, rows, ((c, 0, rows, square),)) for c, column in halves],
        (2, [((0, 1), 0), ((0, 1), 1), ((2, 3), 1), ((2, 3), 0)]),
        [d2["sums"], d3["sums"], d2["ffn_sums"], d3["ffn_sums"]],
    )
    t_rest = sums.add(heights, *rest)
    own_out = jnp.stack([slot(y3, y2), slot(y2, y3)])
    low_grad = jnp.stack([d2[G_LOW], d3[G_LOW]])
    own_grad = jnp.stack([slot(d2["g_in"], d1["g_in"]), slot(d3["g_in"], d2["g_in"])])
    crossed = jnp.stack([slot(r3, r1), slot(r4, r2)])
    got_flip = at.move(tie(crossed, [moved4]), CORE)
    got_swap = at.move(tie(slot(low_grad, own_out), [rest, moved4]), SWAP)
    activations = jnp.where(at.home, own_out, slot(got_swap, got_flip))
    input_grads = jnp.where(at.home, own_grad, slot(got_flip, got_swap).astype(F32))
    moved5 = sums.tick([t_left, t_right], [moved3, moved4])
    sources, numbered = pieces_of([c0, c1, c2])
    taps = call(
        functools.partial(compression_kernel, masks, numbered, square, micro), "compression",
        places(AUTO, *tie(memory, [rest]), *sources),
        [((3 * (n // 2) * square, PAGE), BF, PIN)] * 2,
        [(whole, BF), ((width, PAGE), BF)], 0, base, 2 * SLACK,
    )
    t_comp = sums.add([square] * 3, *taps)
    moved6 = sums.tick([t_rest], [rest])
    moved7 = sums.tick([t_left, t_right, t_rest], [moved5, moved6])
    moved8 = sums.tick([t_comp], [taps, moved6])
    swap0 = sums.finish([t_left], [moved7, got_swap])
    moved9 = sums.tick([t_right, t_rest, t_comp], [moved7, moved8])
    moved10 = sums.tick([t_rest, t_comp], [moved9])
    sums.finish([t_right, t_rest, t_comp], [swap0, moved10])

    def unpage(item, start, count):
        block = item[OUT]
        parts = [block[(start + c) * rows : (start + c + 1) * rows] for c in range(count)]
        return jnp.concatenate(parts, 1)

    def lanes_of(group):
        return group[ITEMS]

    t_left, t_right, t_rest = lanes_of(t_left), lanes_of(t_right), lanes_of(t_rest)
    s_comp = jnp.stack([unpage(item, 0, per) for item in lanes_of(t_comp)])
    spans = (split[0], split[1] - split[0], pages - split[1])
    s_up = jnp.concatenate([unpage(item, 0, span) for item, span in zip(t_left, spans)], 1)
    s_out = unpage(t_left[2], spans[2], per)
    last = t_right[2][OUT]
    s_down = jnp.concatenate(
        [jnp.concatenate([t_right[c][OUT], last[c * (fold - most) : (c + 1) * (fold - most)]], 0) for c, _ in halves], 1
    )
    s_q, s_key, s_value = [unpage(item, 0, per) for item in t_rest]
    s_pos = jnp.concatenate([t_rest[c][OUT][square : square + rows] for c, _ in halves], 1)
    s_vec = t_rest[2][OUT][square:]
    s_norm = jnp.sum(
        q_weight[0].astype(F32) * s_q + key_weight[0].astype(F32) * s_key + value_weight[0].astype(F32) * s_value, 1
    ) / norm_gain[0].astype(F32)
    s_ffn = jnp.sum(up_weight[0].astype(F32) * s_up, 1) / ffn_gain[0].astype(F32)
    outs = (
        activations[:, None], input_grads[:, None], s_q, s_key, s_value, s_pos, s_out, s_up, s_down, s_comp, s_norm,
        s_vec[0, :rows], s_vec[1, :rows], s_ffn, s_vec[3, :fold], s_vec[2, :rows],
    )
    return tuple(o[None] for o in outs)


def solution(mesh):
    rows = P(SECTION, WIDE, None)
    vector = P(SECTION, WIDE)
    stream = P(SECTION, None, WIDE, None, None)
    taps = P(SECTION, None, WIDE, None)
    whole = P(None, WIDE, None, None)
    return jax.shard_map(
        shards,
        mesh=mesh,
        in_specs=(whole, stream, stream, whole) + (rows,) * 7 + (taps,) + (vector,) * 6,
        out_specs=(stream, stream) + (rows,) * 7 + (taps,) + (vector,) * 6,
        check_vma=False,
    )
```
